512 devices in a mesh: gx: 32 (over z, core), gy: 16 (over x, y).
Axes of the slice: x: 4, y: 4, z: 16, core: 2. Of those that a mesh axis runs over, the one named last changes fastest.
Arguments:
- leaf_moments: bfloat16 [131072, 256], P(('gx', 'gy')), may hold values from -6 to 6
- leaf_src: int32 [131072, 32], P(('gx', 'gy')), may hold values from -1 to 4223, as said below
- leaf_cls: int32 [131072, 32], P(('gx', 'gy')), may hold values from -1 to 7
- send_rows: int32 [32, 16, 16, 8], P('gx'), may hold values from 0 to 255, as said below
- send_count: int32 [32, 16, 16], P('gx'), may hold values from 0 to 8, as said below
- par_src: int32 [16384, 32], P(('gx', 'gy')), may hold values from -1 to 16383, as said below
- par_cls: int32 [16384, 32], P(('gx', 'gy')), may hold values from -1 to 7
- top_src: int32 [2048, 32], P('gx'), may hold values from -1 to 63, as said below
- top_cls: int32 [2048, 32], P('gx'), may hold values from -1 to 7
- points: float32 [4096, 3, 128], P(('gx', 'gy')), may hold values from 0 to 1
- charges: float32 [4096, 128], P(('gx', 'gy')), may hold values from -0.18 to 0.18
- near_src: int32 [4096, 8], P(('gx', 'gy')), may hold values from -1 to 4095, as said below
- m2m_ops: bfloat16 [8, 256, 256], replicated, may hold values from -0.125 to 0.125
- m2l_ops: bfloat16 [8, 256, 256], replicated, may hold values from -0.0625 to 0.0625
- l2l_ops: bfloat16 [8, 256, 256], replicated, may hold values from -0.375 to 0.375
Outputs:
- leaf_local: bfloat16 [131072, 256], P(('gx', 'gy'))
- near_potential: float32 [4096, 128], P(('gx', 'gy'))
The draws below stay inside these ranges and needn't reach their ends.
Inputs may be any that keep to these rules, and one draw needn't show every extreme that they name: leaf_src and leaf_cls are -1 in the same slots; a list's used slots come first, at least 16 of them. A value below 4096 names a leaf of the target's own device; a larger one names a sender other than the target's own device. The first send_count[g, s, p] entries of send_rows[g, s, p] are distinct. send_count[g, s, s] = 0; for each device some sender fills all 8 slots. par_src and par_cls are -1 in the same slots; a source parent lies on a device with the same gy index whose gx index differs by at most one. top_src and top_cls are -1 in the same slots. `near_src`: a tile of device d (linear index over gx then gy) lists tiles of global numbers d * 8 - 4 to (d + 1) * 8 + 3, its own tile in slot 0.
All inputs are finite; a program needn't handle non-finite values.
Results may differ from the reference program's by a relative error of at most 0.015.
Values may be sent and summed in bfloat16 or wider, within the bound.
No kernel may reach another device: no remote copies, remote signals or barrier semaphores. Data moves between devices by JAX's collectives and lax.ppermute only.
A program may use at most 64 MiB of HBM per device.

```python
import jax
import jax.numpy as jnp
from jax import lax

P_SIZE = 256
K = 8
LIST = 32
CAP = 8
TILE_PTS = 128
NEAR = 8
HALO_T = 4
LEAF_DEV = 256
TILE_DEV = 8
PAR_DEV = 32
GP_DEV = 4
LEAVES = 131072
PARENTS = 16384
GPS = 2048
TILES = 4096
N_GX = 32
N_GY = 16


def list_mask(key, lead_shape):
    length = jax.random.randint(key, lead_shape, LIST // 2, LIST + 1)
    length = length.at[..., 0].set(LIST).at[..., 1].set(LIST // 2)
    return jnp.arange(LIST) < length[..., None]


def send_tables(key):
    key = jax.random.fold_in(key, 101)
    subkeys = jax.random.split(key, 3)
    scores = jax.random.randint(subkeys[0], (N_GX, N_GY, N_GY, LEAF_DEV), 0, 1 << 18)
    scores = scores * LEAF_DEV + jnp.arange(LEAF_DEV, dtype=jnp.int32)
    chosen = jnp.argsort(scores, axis=-1)[..., :CAP].astype(jnp.int32)
    counts = jax.random.randint(subkeys[1], (N_GX, N_GY, N_GY), 1, CAP + 1)
    filler = jax.random.randint(subkeys[2], (N_GX, 1, N_GY), 1, N_GY)
    sender_ids = jnp.arange(N_GY)[None, :, None]
    receiver_ids = jnp.arange(N_GY)[None, None, :]
    counts = jnp.where(sender_ids == (receiver_ids + filler) % N_GY, CAP, counts)
    counts = jnp.where(sender_ids == receiver_ids, 0, counts)
    return (chosen, counts.astype(jnp.int32))


def leaf_lists(key):
    key = jax.random.fold_in(key, 102)
    subkeys = jax.random.split(key, 6)
    grid_shape = (N_GX, N_GY, LEAF_DEV, LIST)
    usable = list_mask(subkeys[0], (N_GX, N_GY, LEAF_DEV))
    remote = jax.random.randint(subkeys[1], grid_shape, 0, 2) == 1
    local_pick = jax.random.randint(subkeys[2], grid_shape, 0, LEAF_DEV)
    offset = jax.random.randint(subkeys[3], grid_shape, 1, N_GY)
    peer_ids = jnp.arange(N_GY)[None, :, None, None]
    sender_ids = (peer_ids + offset) % N_GY
    slot_pick = jax.random.randint(subkeys[4], grid_shape, 0, CAP)
    remote_code = N_GY * LEAF_DEV + sender_ids * CAP + slot_pick
    source = jnp.where(remote, remote_code, peer_ids * LEAF_DEV + local_pick)
    source = jnp.where(usable, source, -1)
    classes = jnp.where(usable, jax.random.randint(subkeys[5], grid_shape, 0, K), -1)
    return (source.reshape(LEAVES, LIST).astype(jnp.int32), classes.reshape(LEAVES, LIST).astype(jnp.int32))


def parent_lists(key):
    key = jax.random.fold_in(key, 103)
    subkeys = jax.random.split(key, 4)
    grid_shape = (N_GX, N_GY, PAR_DEV, LIST)
    usable = list_mask(subkeys[0], (N_GX, N_GY, PAR_DEV))
    line_ids = jnp.arange(N_GX)[:, None, None, None]
    peer_ids = jnp.arange(N_GY)[None, :, None, None]
    stepping = jax.random.randint(subkeys[1], grid_shape, -1, 2)
    source_line = jnp.clip(line_ids + stepping, 0, N_GX - 1)
    source = (source_line * N_GY + peer_ids) * PAR_DEV + jax.random.randint(subkeys[2], grid_shape, 0, PAR_DEV)
    source = jnp.where(usable, source, -1)
    classes = jnp.where(usable, jax.random.randint(subkeys[3], grid_shape, 0, K), -1)
    return (source.reshape(PARENTS, LIST).astype(jnp.int32), classes.reshape(PARENTS, LIST).astype(jnp.int32))


def top_lists(key):
    key = jax.random.fold_in(key, 104)
    subkeys = jax.random.split(key, 3)
    grid_shape = (N_GX, N_GY * GP_DEV, LIST)
    usable = list_mask(subkeys[0], (N_GX, N_GY * GP_DEV))
    source = jnp.where(usable, jax.random.randint(subkeys[1], grid_shape, 0, N_GY * GP_DEV), -1)
    classes = jnp.where(usable, jax.random.randint(subkeys[2], grid_shape, 0, K), -1)
    return (source.reshape(GPS, LIST).astype(jnp.int32), classes.reshape(GPS, LIST).astype(jnp.int32))


def draw_leaf_src(key, part):
    return leaf_lists(key)[0]


def draw_leaf_cls(key, part):
    return leaf_lists(key)[1]


def draw_send_rows(key, part):
    return send_tables(key)[0]


def draw_send_count(key, part):
    return send_tables(key)[1]


def draw_par_src(key, part):
    return parent_lists(key)[0]


def draw_par_cls(key, part):
    return parent_lists(key)[1]


def draw_top_src(key, part):
    return top_lists(key)[0]


def draw_top_cls(key, part):
    return top_lists(key)[1]


def draw_near_src(key, part):
    key = jax.random.fold_in(key, 105)
    subkeys = jax.random.split(key, 2)
    length = jax.random.randint(subkeys[0], (N_GX * N_GY, TILE_DEV), NEAR // 2, NEAR + 1)
    length = length.at[:, 0].set(NEAR).at[:, 1].set(NEAR // 2)
    usable = jnp.arange(NEAR) < length[..., None]
    device_ids = jnp.arange(N_GX * N_GY)[:, None, None]
    tile_ids = jnp.arange(TILE_DEV)[None, :, None]
    slot_ids = jnp.arange(NEAR)[None, None, :]
    pick = jax.random.randint(subkeys[1], (N_GX * N_GY, TILE_DEV, NEAR), 0, TILE_DEV + 2 * HALO_T)
    source = device_ids * TILE_DEV - HALO_T + pick
    source = jnp.where(slot_ids == 0, device_ids * TILE_DEV + tile_ids, source)
    source = jnp.clip(source, 0, TILES - 1)
    return jnp.where(usable, source, -1).reshape(TILES, NEAR).astype(jnp.int32)


def block_levels(stream_key, dims, cuts, low, top_value):
    level = 1.0
    for axis_at, shards_of in cuts:
        heights = jax.random.uniform(jax.random.fold_in(jax.random.fold_in(stream_key, 6), axis_at), (shards_of,), jnp.float32, low / len(cuts), top_value / len(cuts))
        level = level * jnp.repeat(jnp.exp(heights), dims[axis_at] // shards_of).reshape((-1,) + (1,) * (len(dims) - 1 - axis_at))
    return level


def bell_draw(rng, shape, deviation, limit, pieces=(), kind=jnp.bfloat16):
    factor_of = block_levels(rng, shape, pieces, -0.22, 0.18) if pieces else 1.0
    entries = jax.random.normal(rng, shape, jnp.float32) * deviation * factor_of
    return jnp.minimum(jnp.maximum(entries, -limit), limit).astype(kind)


def setup_inputs(seed: int = 0) -> dict:
    key_list = jax.random.split(jax.random.key(seed), 16)
    return {
        "leaf_moments": bell_draw(key_list[0], (LEAVES, P_SIZE), 1.0, 6.0, ((0, 512),)),
        "leaf_src": draw_leaf_src(jax.random.fold_in(key_list[15], 71), 0),
        "leaf_cls": draw_leaf_cls(jax.random.fold_in(key_list[15], 71), 0),
        "send_rows": draw_send_rows(jax.random.fold_in(key_list[15], 71), 0),
        "send_count": draw_send_count(jax.random.fold_in(key_list[15], 71), 0),
        "par_src": draw_par_src(jax.random.fold_in(key_list[15], 71), 0),
        "par_cls": draw_par_cls(jax.random.fold_in(key_list[15], 71), 0),
        "top_src": draw_top_src(jax.random.fold_in(key_list[15], 71), 0),
        "top_cls": draw_top_cls(jax.random.fold_in(key_list[15], 71), 0),
        "points": jnp.clip(1.0 * jax.random.uniform(key_list[9], (TILES, 3, TILE_PTS), jnp.float32) ** block_levels(key_list[9], (TILES, 3, TILE_PTS), ((0, 512),), -0.2, 0.2), 0.0, 1.0),
        "charges": bell_draw(key_list[10], (TILES, TILE_PTS), 0.03, 0.18, ((0, 512),), jnp.float32),
        "near_src": draw_near_src(jax.random.fold_in(key_list[15], 71), 0),
        "m2m_ops": bell_draw(key_list[12], (8, P_SIZE, P_SIZE), (8 * P_SIZE) ** -0.5, 0.125),
        "m2l_ops": bell_draw(key_list[13], (K, P_SIZE, P_SIZE), (P_SIZE * LIST) ** -0.5, 0.0625),
        "l2l_ops": bell_draw(key_list[14], (8, P_SIZE, P_SIZE), P_SIZE ** -0.5, 0.375),
    }


SOFTENING = 0.05
HIGH = lax.Precision.HIGHEST

def upward(moments, m2m_ops):
    grouped = moments.reshape(-1, 8, moments.shape[1]).astype(jnp.float32)
    summed = jnp.einsum('ncp,cpq->nq', grouped, m2m_ops.astype(jnp.float32), precision=HIGH)
    return summed.astype(jnp.bfloat16)

def downward(locals_in, l2l_ops):
    spread = jnp.einsum('np,cpq->ncq', locals_in.astype(jnp.float32), l2l_ops.astype(jnp.float32), precision=HIGH)
    return spread.reshape(-1, locals_in.shape[1])

def translate(source_bank, row_ids, classes, m2l_ops):
    usable = row_ids >= 0
    picked = jnp.take(source_bank, jnp.clip(row_ids, 0, source_bank.shape[0] - 1), axis=0).astype(jnp.float32)
    onehot = ((classes[..., None] == jnp.arange(m2l_ops.shape[0])) & usable[..., None]).astype(jnp.float32)
    buckets = jnp.einsum('ljk,ljp->klp', onehot, picked, precision=HIGH).astype(jnp.bfloat16)
    return jnp.einsum('klp,kpq->lq', buckets.astype(jnp.float32), m2l_ops.astype(jnp.float32), precision=HIGH)

def level_field(source_bank, row_ids, classes, m2l_ops, per_device):
    row_blocks = row_ids.reshape(-1, per_device, row_ids.shape[-1])
    class_blocks = classes.reshape(-1, per_device, classes.shape[-1])
    result = lax.map(lambda both: translate(source_bank, both[0], both[1], m2l_ops), (row_blocks, class_blocks))
    return result.reshape(-1, source_bank.shape[1])

def leaf_sources(leaf_src, send_rows, send_count):
    row_group = N_GY * LEAF_DEV
    leaf_ids = jnp.arange(leaf_src.shape[0], dtype=jnp.int32)
    line_ids = (leaf_ids // row_group)[:, None]
    peer_ids = (leaf_ids // LEAF_DEV % N_GY)[:, None]
    remote = leaf_src >= row_group
    offset = jnp.clip(leaf_src - row_group, 0, N_GY * CAP - 1).astype(jnp.int32)
    sender = offset // CAP
    slot = offset % CAP
    remote_leaf = send_rows[line_ids, sender, peer_ids, slot]
    live = slot < send_count[line_ids, sender, peer_ids]
    remote_global = line_ids * row_group + sender * LEAF_DEV + remote_leaf
    local_global = line_ids * row_group + leaf_src
    chosen = jnp.where(remote, jnp.where(live, remote_global, -1), local_global)
    return jnp.where(leaf_src < 0, -1, chosen).astype(jnp.int32)

def tile_potential(targets, sources):
    differ_x = targets[:, 0, :, None] - sources[:, 0, None, :]
    differ_y = targets[:, 1, :, None] - sources[:, 1, None, :]
    differ_z = targets[:, 2, :, None] - sources[:, 2, None, :]
    distance_sq = differ_x * differ_x + differ_y * differ_y + differ_z * differ_z
    return lax.optimization_barrier(jnp.sum(sources[:, 3, None, :] * lax.rsqrt(distance_sq + SOFTENING * SOFTENING), axis=-1))

def near_field(points, charges, near_src):
    packed = jnp.concatenate([points, charges[:, None, :]], axis=1)

    def one_device(both):
        targets, lists = both
        running = jnp.zeros((targets.shape[0], targets.shape[2]), jnp.float32)
        for column_index in range(lists.shape[1]):
            column = lists[:, column_index]
            sources = jnp.take(packed, jnp.clip(column, 0, packed.shape[0] - 1), axis=0)
            running = running + jnp.where((column >= 0)[:, None], tile_potential(targets, sources), 0.0)
        return running
    blocks = (points.reshape(-1, TILE_DEV, 3, points.shape[2]), near_src.reshape(-1, TILE_DEV, near_src.shape[1]))
    return lax.map(one_device, blocks).reshape(-1, points.shape[2])

def reference(leaf_moments, leaf_src, leaf_cls, send_rows, send_count, par_src, par_cls, top_src, top_cls, points, charges, near_src, m2m_ops, m2l_ops, l2l_ops):
    parent_moments = upward(leaf_moments, m2m_ops)
    top_moments = upward(parent_moments, m2m_ops)
    top_group = N_GY * GP_DEV
    top_line = jnp.arange(top_moments.shape[0], dtype=jnp.int32) // top_group * top_group
    top_global = jnp.where(top_src >= 0, top_src + top_line[:, None], -1).astype(jnp.int32)
    top_local = level_field(top_moments, top_global, top_cls, m2l_ops, GP_DEV).astype(jnp.bfloat16)
    parent_local = (level_field(parent_moments, par_src, par_cls, m2l_ops, PAR_DEV) + downward(top_local, l2l_ops)).astype(jnp.bfloat16)
    leaf_global = leaf_sources(leaf_src, send_rows, send_count)
    leaf_field = level_field(leaf_moments, leaf_global, leaf_cls, m2l_ops, LEAF_DEV)
    leaf_local = (leaf_field + downward(parent_local, l2l_ops)).astype(jnp.bfloat16)
    near_potential = near_field(points, charges, near_src)
    return (leaf_local, near_potential)
```

```python
import functools

import jax
import jax.numpy as jnp
from jax import lax
from jax.experimental import pallas as pl
from jax.experimental.pallas import tpu as pltpu
from jax.sharding import PartitionSpec as P

F32 = jnp.float32
BF16 = jnp.bfloat16
I32 = jnp.int32

HALO_T = 4
SOFTENING = 0.05
VMEM_LIMIT = 24 * 1024 * 1024


def iota(shape, dim):
    return lax.broadcasted_iota(I32, shape, dim)


def dot(a, b):
    return jnp.dot(a, b, preferred_element_type=F32)


def dot_tn(a, b):
    return lax.dot_general(a, b, (((0,), (0,)), ((), ())), preferred_element_type=F32)


def pack_kernel(leaf_ref, m2m_ref, rows_ref, count_ref, send_ref, parents_ref):
    me = lax.axis_index("gy")
    leaf = leaf_ref[...]
    counts = jnp.broadcast_to(count_ref[pl.ds(me, 1), :].astype(F32), (16, 16))
    counts = jnp.sum(jnp.where(iota((16, 16), 0) == iota((16, 16), 1), counts, 0.0), axis=1, keepdims=True)
    table = rows_ref[me].astype(F32)
    table = jnp.where(iota((16, 8), 1).astype(F32) < counts, table, -1.0).astype(BF16)
    repeat = (iota((128, 16), 0) // 8 == iota((128, 16), 1)).astype(F32).astype(BF16)
    spread = dot(repeat, table)
    column = jnp.sum(
        jnp.where(iota((128, 8), 0) % 8 == iota((128, 8), 1), spread, 0.0), axis=1, keepdims=True
    )
    pick = (iota((128, 256), 1).astype(F32) == column).astype(F32).astype(BF16)
    sent = dot(pick, leaf)
    order = (iota((256, 256), 1) == 8 * (iota((256, 256), 0) % 32) + iota((256, 256), 0) // 32)
    by_child = dot(order.astype(F32).astype(BF16), leaf).astype(BF16)
    parents = dot(by_child[0:32], m2m_ref[0])
    for c in range(1, 8):
        parents += dot(by_child[32 * c : 32 * c + 32], m2m_ref[c])
    parents = parents.astype(BF16)
    parents_ref[...] = parents
    row = iota((64, 32), 0)
    order = (iota((64, 32), 1) == 8 * (row % 8) + row // 8) & (row % 8 < 4)
    by_child = dot(order.astype(F32).astype(BF16), parents)
    top = dot(by_child[0:8].astype(BF16), m2m_ref[0])
    for c in range(1, 8):
        top += dot(by_child[8 * c : 8 * c + 8].astype(BF16), m2m_ref[c])
    for p in range(16):
        send_ref[p] = jnp.concatenate([sent[8 * p : 8 * p + 8], top], axis=0).astype(BF16)


def pack(leaf, m2m, rows, count):
    return pl.pallas_call(
        pack_kernel,
        out_shape=(
            jax.ShapeDtypeStruct((16, 16, 256), BF16),
            jax.ShapeDtypeStruct((32, 256), BF16),
        ),
        compiler_params=pltpu.CompilerParams(vmem_limit_bytes=VMEM_LIMIT),
        cost_estimate=pl.CostEstimate(flops=200_000_000, bytes_accessed=1_500_000, transcendentals=0),
        name="pack",
    )(leaf, m2m, rows, count)


def fields(src_ref, val_ref, lanes, base, rows):
    at = iota((rows, 128), 0)
    even = jnp.zeros((rows, 128), I32)
    odd = jnp.zeros((rows, 128), I32)
    for first, last in ((0, 15), (15, 30), (30, 32)):
        word = jnp.zeros((rows, 128), I32)
        for j in range(first, last):
            hit = at == (src_ref[j : j + 1, lanes] - base)
            word += jnp.where(hit, val_ref[j : j + 1, lanes], 0)
        even += word & 0x0F0F0F0F
        odd += (word >> 4) & 0x0F0F0F0F
    return even, odd


def counts_of(even, odd, k):
    word = odd if k % 2 else even
    return ((word >> (8 * (k // 2))) & 0xFF).astype(F32).astype(BF16)


def lists_kernel(
    leaf_ref, src_ref, cls_ref, par_src_ref, par_cls_ref, top_src_ref, top_cls_ref, m2l_ref,
    partial_ref, far_ref, small_ref,
    src_t, val_t, low_src, low_val, near_w, far_w, z_ref,
):
    me = lax.axis_index("gy")
    device = lax.axis_index("gx") * 16 + me
    src = src_ref[...]
    src = jnp.where(src >= 4096, src - (4096 - 256), src - 256 * me)
    src_t[...] = src.T
    cls = cls_ref[...]
    val_t[...] = jnp.where(cls >= 0, jnp.left_shift(1, 4 * jnp.maximum(cls, 0)), 0).T
    psrc = par_src_ref[...]
    place = (psrc // 32 - device + 16) // 16
    psrc = jnp.where(psrc >= 0, place * 32 + psrc % 32, -1)
    tsrc = top_src_ref[pl.ds(4 * me, 4), :]
    tsrc = jnp.where(tsrc >= 0, (tsrc // 4) * 8 + tsrc % 4, -1)
    tcls = top_cls_ref[pl.ds(4 * me, 4), :]
    both = jnp.concatenate([psrc, tsrc, jnp.full((92, 32), -1, I32)], axis=0)
    low_src[...] = both.T
    both = jnp.concatenate([par_cls_ref[...], tcls, jnp.full((92, 32), -1, I32)], axis=0)
    low_val[...] = jnp.where(both >= 0, jnp.left_shift(1, 4 * jnp.maximum(both, 0)), 0).T

    rows = 64

    def near_block(i, _):
        for half in range(2):
            lanes = slice(128 * half, 128 * half + 128)
            even, odd = fields(src_t, val_t, lanes, i * rows, rows)
            for k in range(8):
                near_w[pl.ds(pl.multiple_of(256 * k + i * rows, rows), rows), lanes] = counts_of(even, odd, k)
        return 0

    def far_block(i, _):
        for half in range(2):
            lanes = slice(128 * half, 128 * half + 128)
            even, odd = fields(src_t, val_t, lanes, 256 + i * rows, rows)
            for k in range(8):
                far_w[pl.ds(pl.multiple_of(128 * k + i * rows, rows), rows), lanes] = counts_of(even, odd, k)
        return 0

    def small_block(i, _):
        even, odd = fields(low_src, low_val, slice(0, 128), i * rows, rows)
        for k in range(8):
            small_ref[k, pl.ds(pl.multiple_of(i * rows, rows), rows), :] = counts_of(even, odd, k)
        return 0

    lax.fori_loop(0, 4, near_block, 0)
    lax.fori_loop(0, 2, far_block, 0)
    lax.fori_loop(0, 2, small_block, 0)

    leaf = leaf_ref[...]
    for k in range(8):
        z_ref[256 * k : 256 * k + 256, :] = dot(leaf, m2l_ref[k]).astype(BF16)
    partial_ref[...] = dot_tn(near_w[...], z_ref[...])
    for k in range(8):
        far_ref[:, 128 * k : 128 * k + 128] = far_w[128 * k : 128 * k + 128, :].T


def lists(leaf, src, cls, par_src, par_cls, top_src, top_cls, m2l):
    return pl.pallas_call(
        lists_kernel,
        out_shape=(
            jax.ShapeDtypeStruct((256, 256), F32),
            jax.ShapeDtypeStruct((256, 1024), BF16),
            jax.ShapeDtypeStruct((8, 128, 128), BF16),
        ),
        scratch_shapes=[
            pltpu.VMEM((32, 256), I32),
            pltpu.VMEM((32, 256), I32),
            pltpu.VMEM((32, 128), I32),
            pltpu.VMEM((32, 128), I32),
            pltpu.VMEM((2048, 256), BF16),
            pltpu.VMEM((1024, 256), BF16),
            pltpu.VMEM((2048, 256), BF16),
        ],
        compiler_params=pltpu.CompilerParams(vmem_limit_bytes=VMEM_LIMIT),
        cost_estimate=pl.CostEstimate(flops=3_000_000_000, bytes_accessed=2_500_000, transcendentals=0),
        name="lists",
    )(leaf, src, cls, par_src, par_cls, top_src, top_cls, m2l)


def pieces(x):
    high = x.astype(BF16).astype(F32)
    rest = x - high
    middle = rest.astype(BF16).astype(F32)
    return high, middle, rest - middle


def near_kernel(list_ref, points_ref, charges_ref, below_ref, above_ref, out_ref, source_s, target_s, q_s):
    device = lax.axis_index("gx") * 16 + lax.axis_index("gy")
    ones = jnp.ones((3, 128), F32)
    pad = jnp.zeros((5, 128), F32)
    for s in range(16):
        if s < 4:
            xyz, q = below_ref[s, 0:3, :], below_ref[s, 3:4, :]
        elif s < 12:
            xyz, q = points_ref[s - 4], charges_ref[s - 4 : s - 3, :]
        else:
            xyz, q = above_ref[s - 12, 0:3, :], above_ref[s - 12, 3:4, :]
        q_s[s] = jnp.broadcast_to(q, (8, 128))
        high, middle, low = pieces(xyz)
        norm = jnp.sum(xyz * xyz, axis=0, keepdims=True)
        n = jnp.concatenate(pieces(norm), axis=0)
        source_s[s] = jnp.concatenate(
            [high, high, middle, high, low, middle, ones, n, jnp.zeros((8, 128), F32)], axis=0
        ).astype(BF16)
        if 4 <= s < 12:
            n = jnp.concatenate(pieces(norm + SOFTENING * SOFTENING), axis=0)
            target_s[s - 4] = jnp.concatenate(
                [-2.0 * high, -2.0 * middle, -2.0 * high, -2.0 * low, -2.0 * high, -2.0 * middle, n, ones,
                 jnp.zeros((8, 128), F32)],
                axis=0,
            ).astype(BF16)

    def tile(t, _):
        target = target_s[t]
        total = jnp.zeros((128, 128), F32)
        for j in range(8):
            number = list_ref[t, j]
            place = jnp.clip(number - (device * 8 - HALO_T), 0, 15)
            q = q_s[place][0:1, :] * jnp.where(number >= 0, 1.0, 0.0)
            total += q * lax.rsqrt(dot_tn(target, source_s[place]))
        out_ref[pl.ds(t, 1), :] = jnp.sum(total.T, axis=0, keepdims=True)
        return 0

    lax.fori_loop(0, 8, tile, 0)


def near(near_src, points, charges, below, above):
    vmem = pl.BlockSpec(memory_space=pltpu.VMEM)
    return pl.pallas_call(
        near_kernel,
        out_shape=jax.ShapeDtypeStruct((8, 128), F32),
        in_specs=[pl.BlockSpec(memory_space=pltpu.SMEM), vmem, vmem, vmem, vmem],
        scratch_shapes=[
            pltpu.VMEM((16, 32, 128), BF16),
            pltpu.VMEM((8, 32, 128), BF16),
            pltpu.VMEM((16, 8, 128), F32),
        ],
        compiler_params=pltpu.CompilerParams(vmem_limit_bytes=VMEM_LIMIT),
        cost_estimate=pl.CostEstimate(flops=1_500_000_000, bytes_accessed=100_000, transcendentals=1_000_000),
        name="near",
    )(near_src, points, charges, below, above)


def down_kernel(
    recv_ref, before_ref, parents_ref, after_ref, partial_ref, far_ref, small_ref, m2l_ref, l2l_ref,
    out_ref, far_z, top_z, par_z,
):
    recv = recv_ref[...].reshape(256, 256)
    bank = jnp.concatenate([before_ref[...], parents_ref[...], after_ref[...]], axis=0)
    for k in range(8):
        z = dot(recv, m2l_ref[k]).reshape(16, 16, 256)
        far_z[128 * k : 128 * k + 128, :] = z[:, :8].reshape(128, 256).astype(BF16)
        top_z[128 * k : 128 * k + 128, :] = z[:, 8:].reshape(128, 256).astype(BF16)
        z = dot(bank, m2l_ref[k])
        par_z[128 * k : 128 * k + 128, :] = jnp.concatenate([z, jnp.zeros((32, 256), F32)], axis=0).astype(BF16)
    weights = small_ref[...].reshape(1024, 128)
    top_field = dot_tn(weights, top_z[...])
    top_local = top_field.astype(BF16)
    par_field = dot_tn(weights, par_z[...])[0:32]
    row = iota((32, 128), 0)
    lane = iota((32, 128), 1)
    for c in range(8):
        spread = ((lane == 32 + row // 8) & (row % 8 == c)).astype(F32).astype(BF16)
        par_field += dot(dot(spread, top_local).astype(BF16), l2l_ref[c])
    parent_local = par_field.astype(BF16)
    total = partial_ref[...] + dot(far_ref[...], far_z[...])
    row = iota((256, 32), 0)
    lane = iota((256, 32), 1)
    for c in range(8):
        spread = ((lane == row // 8) & (row % 8 == c)).astype(F32).astype(BF16)
        total += dot(dot(spread, parent_local).astype(BF16), l2l_ref[c])
    out_ref[...] = total.astype(BF16)


def down(recv, before, parents, after, partial, far, small, m2l, l2l):
    return pl.pallas_call(
        down_kernel,
        out_shape=jax.ShapeDtypeStruct((256, 256), BF16),
        scratch_shapes=[
            pltpu.VMEM((1024, 256), BF16),
            pltpu.VMEM((1024, 256), BF16),
            pltpu.VMEM((1024, 256), BF16),
        ],
        compiler_params=pltpu.CompilerParams(vmem_limit_bytes=VMEM_LIMIT),
        cost_estimate=pl.CostEstimate(flops=1_500_000_000, bytes_accessed=3_500_000, transcendentals=0),
        name="down",
    )(recv, before, parents, after, partial, far, small, m2l, l2l)


def shifted(block, axes, distance):
    size = lax.axis_size(axes)
    route = [(i, i + distance) for i in range(size) if 0 <= i + distance < size]
    return lax.ppermute(block, axes, route)


def per_device(
    leaf_moments, leaf_src, leaf_cls, send_rows, send_count, par_src, par_cls, top_src, top_cls,
    points, charges, near_src, m2m_ops, m2l_ops, l2l_ops,
):
    packed = jnp.concatenate([points, charges[:, None, :]], axis=1)
    below = shifted(packed[-HALO_T:], ("gx", "gy"), 1)
    above = shifted(packed[:HALO_T], ("gx", "gy"), -1)
    sent, parents = pack(leaf_moments, m2m_ops, send_rows[0], send_count[0])
    recv = lax.all_to_all(sent, "gy", 0, 0, tiled=True)
    before = shifted(parents, "gx", 1)
    after = shifted(parents, "gx", -1)
    partial, far, small = lists(leaf_moments, leaf_src, leaf_cls, par_src, par_cls, top_src, top_cls, m2l_ops)
    near_total = near(near_src, points, charges, below, above)
    leaf_local = down(recv, before, parents, after, partial, far, small, m2l_ops, l2l_ops)
    return leaf_local, near_total


def solution(mesh):
    both = P(("gx", "gy"))
    return jax.shard_map(
        per_device,
        mesh=mesh,
        in_specs=(both, both, both, P("gx"), P("gx"), both, both, P("gx"), P("gx"), both, both, both, P(), P(), P()),
        out_specs=(both, both),
        check_vma=False,
    )
```

```python
import jax
import jax.numpy as jnp
from jax import lax
from jax.experimental import pallas as pl
from jax.experimental.pallas import tpu as pltpu
from jax.sharding import PartitionSpec as P

F32 = jnp.float32
BF16 = jnp.bfloat16
I32 = jnp.int32

HALO_T = 4
SOFTENING = 0.05
VMEM_LIMIT = 10 * 1024 * 1024
PACK_VMEM = 60 * 1024 * 1024


def iota(shape, dim):
    return lax.broadcasted_iota(I32, shape, dim)


def dot(a, b):
    return jnp.dot(a, b, preferred_element_type=F32)


def dot_nt(a, b):
    return lax.dot_general(a, b, (((1,), (1,)), ((), ())), preferred_element_type=F32)


def dot_tn(a, b):
    return lax.dot_general(a, b, (((0,), (0,)), ((), ())), preferred_element_type=F32)


def pieces(x):
    high = x.astype(BF16).astype(F32)
    rest = x - high
    middle = rest.astype(BF16).astype(F32)
    return high, middle, rest - middle


def wide(value):
    return jnp.concatenate([value[0], value[1]], axis=1)


def every_eighth(ref, first, count):
    return wide([ref[half, pl.ds(first, count, stride=8), :] for half in range(2)])


def put_every_eighth(ref, first, count, value):
    for half in range(2):
        ref[half, pl.ds(first, count, stride=8), :] = value[:, 128 * half : 128 * half + 128]


def fetch(copies):
    for copy in copies:
        copy.start()
    return copies


def tile_rows(parts, first):
    left = jnp.concatenate([part[first : first + HALO_T] for part in parts[:6]], axis=0)
    right = jnp.concatenate([part[first : first + HALO_T] for part in parts[6:]], axis=0)
    return jnp.concatenate([jnp.concatenate([left, right], axis=1), jnp.zeros((8, 256), F32)], axis=0)


def pack_kernel(
    leaf_hbm, m2m_hbm, rows_hbm, count_hbm, points_hbm, charges_hbm, send_ref, parents_ref,
    leaf_ref, m2m_ref, rows_ref, count_ref, points_ref, charges_ref, leaf_s, parents_s, sems,
):
    me = lax.axis_index("gy")
    pairs = (
        (leaf_hbm, leaf_ref), (rows_hbm.at[me], rows_ref), (count_hbm, count_ref),
        (points_hbm, points_ref), (charges_hbm, charges_ref), (m2m_hbm, m2m_ref),
    )
    copies = fetch([pltpu.make_async_copy(a, b, sems.at[i]) for i, (a, b) in enumerate(pairs)])
    parents_s[:, 32:64, :] = jnp.zeros((2, 32, 128), F32)
    for copy in copies[:5]:
        copy.wait()
    leaf = leaf_ref[...]
    for half in range(2):
        leaf_s[half] = leaf[:, 128 * half : 128 * half + 128].astype(F32)
    table = rows_ref[...].astype(F32)
    live = iota((8, 16), 0) < count_ref[pl.ds(me, 1), :]
    table = jnp.where(live, table, -1.0).astype(BF16)
    repeat = (iota((128, 16), 0) // 8 == iota((128, 16), 1)).astype(F32).astype(BF16)
    spread = dot_nt(repeat, table)
    column = jnp.sum(
        jnp.where(iota((128, 8), 0) % 8 == iota((128, 8), 1), spread, 0.0), axis=1, keepdims=True
    )
    pick = (iota((128, 256), 1).astype(F32) == column).astype(F32).astype(BF16)
    sent = dot(pick, leaf)
    parts = [[], [], []]
    for axis in range(3):
        for kind, part in enumerate(pieces(points_ref[axis])):
            parts[kind].append(part)
    parts = parts[0] + parts[1] + parts[2] + list(pieces(charges_ref[...]))
    first = tile_rows(parts, 0)
    last = tile_rows(parts, 8 - HALO_T)
    copies[5].wait()
    parents = jnp.zeros((32, 256), F32)
    for c in range(8):
        parents += dot(every_eighth(leaf_s, c, 32).astype(BF16), m2m_ref[c])
    parents = parents.astype(BF16)
    parents_ref[...] = parents
    for half in range(2):
        parents_s[half, 0:32, :] = parents[:, 128 * half : 128 * half + 128].astype(F32)
    top = jnp.zeros((8, 256), F32)
    for c in range(8):
        top += dot(every_eighth(parents_s, c, 8).astype(BF16), m2m_ref[c])
    for p in range(16):
        tiles = jnp.where(me + 1 == p, last, jnp.where(me - 1 == p, first, 0.0))
        send_ref[p] = jnp.concatenate([sent[8 * p : 8 * p + 8], top, tiles], axis=0).astype(BF16)


def pack(leaf, m2m, rows, count, points, charges):
    return pl.pallas_call(
        pack_kernel,
        out_shape=(
            jax.ShapeDtypeStruct((16, 48, 256), BF16),
            jax.ShapeDtypeStruct((32, 256), BF16),
        ),
        in_specs=[pl.BlockSpec(memory_space=pltpu.HBM)] * 6,
        scratch_shapes=[
            pltpu.VMEM((256, 256), BF16),
            pltpu.VMEM((8, 256, 256), BF16),
            pltpu.VMEM((8, 16), I32),
            pltpu.VMEM((16, 16), I32),
            pltpu.VMEM((3, 8, 128), F32),
            pltpu.VMEM((8, 128), F32),
            pltpu.VMEM((2, 256, 128), F32),
            pltpu.VMEM((2, 64, 128), F32),
            pltpu.SemaphoreType.DMA((6,)),
        ],
        compiler_params=pltpu.CompilerParams(vmem_limit_bytes=PACK_VMEM),
        cost_estimate=pl.CostEstimate(flops=200_000_000, bytes_accessed=1_500_000, transcendentals=0),
        name="pack",
    )(leaf, m2m, rows, count, points, charges)


def fields(src_ref, val_ref, lanes, base, rows):
    at = iota((rows, 128), 0)
    even = jnp.zeros((rows, 128), I32)
    odd = jnp.zeros((rows, 128), I32)
    for first, last in ((0, 15), (15, 30), (30, 32)):
        word = jnp.zeros((rows, 128), I32)
        for j in range(first, last):
            hit = at == (src_ref[j : j + 1, lanes] - base)
            word += jnp.where(hit, val_ref[j : j + 1, lanes], 0)
        even += word & 0x0F0F0F0F
        odd += (word >> 4) & 0x0F0F0F0F
    return even, odd


def counts_of(even, odd, k):
    word = odd if k % 2 else even
    return ((word >> (8 * (k // 2))) & 0xFF).astype(F32).astype(BF16)


def field_of(cls):
    return jnp.where(cls >= 0, jnp.left_shift(1, 4 * jnp.maximum(cls, 0)), 0)


def lists_kernel(
    leaf_ref, m2l_ref, before_ref, parents_ref, after_ref, src_hbm, cls_hbm, par_src_hbm, par_cls_hbm, top_src_hbm, top_cls_hbm,
    partial_ref, far_ref, par_ref, top_ref,
    src_t, val_t, low_src, low_val, par_src_ref, par_cls_ref, top_src_ref, top_cls_ref, near_w, far_w, z_ref, small_w, par_z, sems,
):
    me = lax.axis_index("gy")
    device = lax.axis_index("gx") * 16 + me
    pairs = (
        (src_hbm, src_t), (cls_hbm, val_t), (par_src_hbm, par_src_ref), (par_cls_hbm, par_cls_ref),
        (top_src_hbm, top_src_ref), (top_cls_hbm, top_cls_ref),
    )
    copies = fetch([pltpu.make_async_copy(a, b, sems.at[i]) for i, (a, b) in enumerate(pairs)])
    leaf = leaf_ref[...]
    for k in range(8):
        z_ref[256 * k : 256 * k + 256, :] = dot(leaf, m2l_ref[k]).astype(BF16)
    bank = jnp.concatenate([before_ref[...], parents_ref[...], after_ref[...]], axis=0)
    for k in range(8):
        z = dot(bank, m2l_ref[k])
        par_z[128 * k : 128 * k + 128, :] = jnp.concatenate([z, jnp.zeros((32, 256), F32)], axis=0).astype(BF16)
    for copy in copies:
        copy.wait()
    src = src_t[...]
    src_t[...] = jnp.where(src >= 4096, src - (4096 - 256), src - 256 * me)
    val_t[...] = field_of(val_t[...])
    src = par_src_ref[...]
    place = (src // 32 - device + 16) // 16
    src = jnp.where(src >= 0, place * 32 + src % 32, -1)
    none = jnp.full((96, 32), -1, I32)
    src = jnp.concatenate([src, none], axis=0).T
    cls = jnp.concatenate([par_cls_ref[...], none], axis=0).T
    top = top_src_ref[...]
    top = jnp.where(top >= 0, (top // 4) * 8 + top % 4, -1)
    none = jnp.full((32, 32), -1, I32)
    low_src[...] = jnp.concatenate([src[:, 0:32], top, none], axis=1)
    low_val[...] = field_of(jnp.concatenate([cls[:, 0:32], top_cls_ref[...], none], axis=1))

    rows = 64

    def near_block(i, _):
        for half in range(2):
            lanes = slice(128 * half, 128 * half + 128)
            even, odd = fields(src_t, val_t, lanes, i * rows, rows)
            for k in range(8):
                near_w[pl.ds(pl.multiple_of(256 * k + i * rows, rows), rows), lanes] = counts_of(even, odd, k)
        return 0

    def far_block(i, _):
        for half in range(2):
            lanes = slice(128 * half, 128 * half + 128)
            even, odd = fields(src_t, val_t, lanes, 256 + i * rows, rows)
            for k in range(8):
                far_w[pl.ds(pl.multiple_of(128 * k + i * rows, rows), rows), lanes] = counts_of(even, odd, k)
        return 0

    def small_block(i, _):
        even, odd = fields(low_src, low_val, slice(0, 128), i * rows, rows)
        for k in range(8):
            small_w[pl.ds(pl.multiple_of(128 * k + i * rows, rows), rows), :] = counts_of(even, odd, k)
        return 0

    lax.fori_loop(0, 4, near_block, 0)
    lax.fori_loop(0, 2, far_block, 0)
    lax.fori_loop(0, 2, small_block, 0)
    partial_ref[...] = dot_tn(near_w[...], z_ref[...])
    for k in range(8):
        far_ref[:, 128 * k : 128 * k + 128] = far_w[128 * k : 128 * k + 128, :].T
    weights = small_w[...].T
    top_ref[...] = weights
    par_ref[...] = dot(weights[0:32], par_z[...])


def lists(leaf, m2l, before, parents, after, src, cls, par_src, par_cls, top_src, top_cls):
    vmem = pl.BlockSpec(memory_space=pltpu.VMEM)
    return pl.pallas_call(
        lists_kernel,
        out_shape=(
            jax.ShapeDtypeStruct((256, 256), F32),
            jax.ShapeDtypeStruct((256, 1024), BF16),
            jax.ShapeDtypeStruct((32, 256), F32),
            jax.ShapeDtypeStruct((128, 1024), BF16),
        ),
        in_specs=[vmem] * 5 + [pl.BlockSpec(memory_space=pltpu.HBM)] * 6,
        scratch_shapes=[
            pltpu.VMEM((32, 256), I32),
            pltpu.VMEM((32, 256), I32),
            pltpu.VMEM((32, 128), I32),
            pltpu.VMEM((32, 128), I32),
            pltpu.VMEM((32, 32), I32),
            pltpu.VMEM((32, 32), I32),
            pltpu.VMEM((32, 64), I32),
            pltpu.VMEM((32, 64), I32),
            pltpu.VMEM((2048, 256), BF16),
            pltpu.VMEM((1024, 256), BF16),
            pltpu.VMEM((2048, 256), BF16),
            pltpu.VMEM((1024, 128), BF16),
            pltpu.VMEM((1024, 256), BF16),
            pltpu.SemaphoreType.DMA((6,)),
        ],
        compiler_params=pltpu.CompilerParams(vmem_limit_bytes=VMEM_LIMIT),
        cost_estimate=pl.CostEstimate(flops=4_000_000_000, bytes_accessed=2_500_000, transcendentals=0),
        name="lists",
    )(leaf, m2l, before, parents, after, src, cls, par_src, par_cls, top_src, top_cls)


def near_kernel(
    list_ref, points_ref, charges_ref, recv_ref, edge_ref, out_ref, source_s, target_s, source_b, q_s, total_s
):
    me = lax.axis_index("gy")
    device = lax.axis_index("gx") * 16 + me
    source_s[...] = jnp.zeros_like(source_s)
    target_s[...] = jnp.zeros_like(target_s)

    def put(ref, first, count, row, value):
        ref[pl.ds(32 * first + row, count, stride=32), :] = value

    def put_source(first, count, xyz, q):
        for kind_row, kind in enumerate((0, 0, 1, 0, 2, 1)):
            for axis in range(3):
                put(source_s, first, count, 3 * kind_row + axis, xyz[kind][axis])
        norm = 0.0
        for axis in range(3):
            whole = xyz[0][axis] + xyz[1][axis] + xyz[2][axis]
            norm += whole * whole
        for i, part in enumerate(pieces(norm)):
            put(source_s, first, count, 18 + i, jnp.ones((count, 128), F32))
            put(source_s, first, count, 21 + i, part)
        q_s[first : first + count, :] = q
        return norm

    below = recv_ref[jnp.maximum(me - 1, 0), 16:48, :].astype(F32)
    above = recv_ref[jnp.minimum(me + 1, 15), 16:48, :].astype(F32)
    far = [edge_ref[axis] for axis in range(4)]
    for first, rows, start, end in ((0, below, 4, me == 0), (12, above, 0, me == 15)):
        parts = [rows[4 * (i % 6) : 4 * (i % 6) + 4, 128 * (i // 6) : 128 * (i // 6) + 128] for i in range(12)]
        other = [pieces(far[axis][start : start + 4]) for axis in range(3)]
        xyz = [[jnp.where(end, other[axis][kind], parts[3 * kind + axis]) for axis in range(3)] for kind in range(3)]
        put_source(first, 4, xyz, jnp.where(end, far[3][start : start + 4], parts[9] + parts[10] + parts[11]))
    split = [pieces(points_ref[axis]) for axis in range(3)]
    xyz = [[split[axis][kind] for axis in range(3)] for kind in range(3)]
    norm = put_source(4, 8, xyz, charges_ref[...])
    for kind_row, kind in enumerate((0, 1, 0, 2, 0, 1)):
        for axis in range(3):
            put(target_s, 0, 8, 3 * kind_row + axis, -2.0 * xyz[kind][axis])
    for i, part in enumerate(pieces(norm + SOFTENING * SOFTENING)):
        put(target_s, 0, 8, 18 + i, part)
        put(target_s, 0, 8, 21 + i, jnp.ones((8, 128), F32))
    for s in range(16):
        source_b[s] = source_s[32 * s : 32 * s + 32, :].astype(BF16)

    def tile(t, _):
        target = target_s[pl.ds(pl.multiple_of(32 * t, 32), 32), :].T.astype(BF16)
        total = jnp.zeros((128, 128), F32)
        for j in range(0, 8, 2):
            sources, weights = [], []
            for i in (j, j + 1):
                number = list_ref[t, i]
                place = jnp.clip(number - (device * 8 - HALO_T), 0, 15)
                sources.append(source_b[place])
                weights.append(q_s[pl.ds(place, 1), :] * jnp.where(number >= 0, 1.0, 0.0))
            square = dot(target, jnp.concatenate(sources, axis=1))
            total += weights[0] * lax.rsqrt(square[:, 0:128]) + weights[1] * lax.rsqrt(square[:, 128:256])
        out_ref[pl.ds(t, 1), :] = jnp.sum(total.T, axis=0, keepdims=True)
        return 0

    lax.fori_loop(0, 8, tile, 0)


def near(near_src, points, charges, recv, edge):
    vmem = pl.BlockSpec(memory_space=pltpu.VMEM)
    return pl.pallas_call(
        near_kernel,
        out_shape=jax.ShapeDtypeStruct((8, 128), F32),
        in_specs=[pl.BlockSpec(memory_space=pltpu.SMEM), vmem, vmem, vmem, vmem],
        scratch_shapes=[
            pltpu.VMEM((512, 128), F32),
            pltpu.VMEM((256, 128), F32),
            pltpu.VMEM((16, 32, 128), BF16),
            pltpu.VMEM((16, 128), F32),
            pltpu.VMEM((128, 128), F32),
        ],
        compiler_params=pltpu.CompilerParams(vmem_limit_bytes=VMEM_LIMIT),
        cost_estimate=pl.CostEstimate(flops=1_500_000_000, bytes_accessed=100_000, transcendentals=1_000_000),
        name="near",
    )(near_src, points, charges, recv, edge)


def down_kernel(
    recv_ref, partial_ref, far_ref, par_ref, top_ref, m2l_ref, l2l_ref,
    out_ref, far_z, top_z, parents_s, leaves_s,
):
    me = lax.axis_index("gy")
    recv = jnp.concatenate([recv_ref[s, 0:16, :] for s in range(16)], axis=0)
    for k in range(8):
        z = dot(recv, m2l_ref[k]).reshape(16, 16, 256)
        far_z[128 * k : 128 * k + 128, :] = z[:, :8].reshape(128, 256).astype(BF16)
        top_z[128 * k : 128 * k + 128, :] = z[:, 8:].reshape(128, 256).astype(BF16)
    top_local = dot(top_ref[...], top_z[...]).astype(BF16)
    own = (iota((8, 128), 1) == 32 + 4 * me + iota((8, 128), 0)) & (iota((8, 128), 0) < 4)
    top_local = dot(own.astype(F32).astype(BF16), top_local).astype(BF16)
    for c in range(8):
        put_every_eighth(parents_s, c, 4, dot(top_local, l2l_ref[c])[0:4])
    parent_local = (par_ref[...] + wide(parents_s[...])).astype(BF16)
    for c in range(8):
        put_every_eighth(leaves_s, c, 32, dot(parent_local, l2l_ref[c]))
    total = partial_ref[...] + dot(far_ref[...], far_z[...])
    out_ref[...] = (total + wide(leaves_s[...])).astype(BF16)


def down(recv, partial, far, par, top, m2l, l2l):
    return pl.pallas_call(
        down_kernel,
        out_shape=jax.ShapeDtypeStruct((256, 256), BF16),
        scratch_shapes=[
            pltpu.VMEM((1024, 256), BF16),
            pltpu.VMEM((1024, 256), BF16),
            pltpu.VMEM((2, 32, 128), F32),
            pltpu.VMEM((2, 256, 128), F32),
        ],
        compiler_params=pltpu.CompilerParams(vmem_limit_bytes=VMEM_LIMIT),
        cost_estimate=pl.CostEstimate(flops=1_500_000_000, bytes_accessed=3_500_000, transcendentals=0),
        name="down",
    )(recv, partial, far, par, top, m2l, l2l)


def shifted(block, axis, distance):
    size = lax.axis_size(axis)
    route = [(i, i + distance) for i in range(size) if 0 <= i + distance < size]
    return lax.ppermute(block, axis, route)


def across(block):
    rows, width = lax.axis_size("gx"), lax.axis_size("gy")
    ends = [(g * width + width - 1, (g + 1) * width) for g in range(rows - 1)]
    return lax.ppermute(block, ("gx", "gy"), ends + [(b, a) for a, b in ends])


def per_device(
    leaf_moments, leaf_src, leaf_cls, send_rows, send_count, par_src, par_cls, top_src, top_cls,
    points, charges, near_src, m2m_ops, m2l_ops, l2l_ops,
):
    points = points.transpose(1, 0, 2)
    edge = across(jnp.concatenate([points, charges[None]], axis=0))
    sent, parents = pack(
        leaf_moments, m2m_ops, send_rows[0].transpose(0, 2, 1), send_count[0], points, charges
    )
    before = shifted(parents, "gx", 1)
    after = shifted(parents, "gx", -1)
    recv = lax.all_to_all(sent, "gy", 0, 0, tiled=True)
    partial, far, par, top = lists(
        leaf_moments, m2l_ops, before, parents, after,
        leaf_src.T, leaf_cls.T, par_src, par_cls, top_src.T, top_cls.T,
    )
    leaf_local = down(recv, partial, far, par, top, m2l_ops, l2l_ops)
    near_total = near(near_src, points, charges, recv, edge)
    return leaf_local, near_total


def solution(mesh):
    both = P(("gx", "gy"))
    return jax.shard_map(
        per_device,
        mesh=mesh,
        in_specs=(both, both, both, P("gx"), P("gx"), both, both, P("gx"), P("gx"), both, both, both, P(), P(), P()),
        out_specs=(both, both),
        check_vma=False,
    )
```

```python
import jax
import jax.numpy as jnp
from jax import lax
from jax.experimental import pallas as pl
from jax.experimental.pallas import tpu as pltpu
from jax.sharding import PartitionSpec as P

F32 = jnp.float32
BF16 = jnp.bfloat16
I32 = jnp.int32

HALO_T = 4
SOFTENING = 0.05
VMEM_LIMIT = 10 * 1024 * 1024
PACK_VMEM = 60 * 1024 * 1024


def iota(shape, dim):
    return lax.broadcasted_iota(I32, shape, dim)


def dot(a, b):
    return jnp.dot(a, b, preferred_element_type=F32)


def dot_nt(a, b):
    return lax.dot_general(a, b, (((1,), (1,)), ((), ())), preferred_element_type=F32)


def dot_tn(a, b):
    return lax.dot_general(a, b, (((0,), (0,)), ((), ())), preferred_element_type=F32)


def pieces(x):
    high = x.astype(BF16).astype(F32)
    rest = x - high
    middle = rest.astype(BF16).astype(F32)
    return high, middle, rest - middle


def wide(value):
    return jnp.concatenate([value[0], value[1]], axis=1)


def every_eighth(ref, first, count):
    return wide([ref[half, pl.ds(first, count, stride=8), :] for half in range(2)])


def put_every_eighth(ref, first, count, value):
    for half in range(2):
        ref[half, pl.ds(first, count, stride=8), :] = value[:, 128 * half : 128 * half + 128]


def fetch(copies):
    for copy in copies:
        copy.start()
    return copies


def tile_rows(parts, first):
    high = jnp.concatenate([part[0][first : first + HALO_T] for part in parts], axis=0)
    rest = jnp.concatenate([part[1][first : first + HALO_T] for part in parts], axis=0)
    return jnp.concatenate([high, rest], axis=1)


def pack_kernel(
    leaf_hbm, m2m_hbm, rows_hbm, count_hbm, points_hbm, charges_hbm, send_hbm, parents_hbm, edge_hbm,
    leaf_ref, m2m_ref, rows_ref, count_ref, points_ref, charges_ref, leaf_s, parents_s, send_ref, parents_ref, edge_ref, sems,
):
    me = lax.axis_index("gy")
    pairs = (
        (leaf_hbm, leaf_ref), (rows_hbm.at[me], rows_ref), (count_hbm, count_ref),
        (points_hbm, points_ref), (charges_hbm, charges_ref), (m2m_hbm, m2m_ref),
    )
    copies = fetch([pltpu.make_async_copy(a, b, sems.at[i]) for i, (a, b) in enumerate(pairs)])
    parents_s[:, 32:64, :] = jnp.zeros((2, 32, 128), F32)
    for copy in copies[:5]:
        copy.wait()
    leaf = leaf_ref[...]
    for half in range(2):
        leaf_s[half] = leaf[:, 128 * half : 128 * half + 128].astype(F32)
    table = rows_ref[...].astype(F32)
    live = iota((8, 16), 0) < count_ref[pl.ds(me, 1), :]
    table = jnp.where(live, table, -1.0).astype(BF16)
    repeat = (iota((128, 16), 0) // 8 == iota((128, 16), 1)).astype(F32).astype(BF16)
    spread = dot_nt(repeat, table)
    column = jnp.sum(
        jnp.where(iota((128, 8), 0) % 8 == iota((128, 8), 1), spread, 0.0), axis=1, keepdims=True
    )
    pick = (iota((128, 256), 1).astype(F32) == column).astype(F32).astype(BF16)
    sent = dot(pick, leaf)
    parts = [pieces(x) for x in (points_ref[0], points_ref[1], points_ref[2], charges_ref[...])]
    edge_ref[0:3] = points_ref[...]
    edge_ref[3] = charges_ref[...]
    first = tile_rows(parts, 0)
    last = tile_rows(parts, 8 - HALO_T)
    for p in range(16):
        tiles = jnp.where(me + 1 == p, last, jnp.where(me - 1 == p, first, 0.0))
        send_ref[p, 16:32, :] = tiles.astype(BF16)
    stores = fetch([
        pltpu.make_async_copy(edge_ref, edge_hbm, sems.at[6]),
        pltpu.make_async_copy(send_ref.at[:, 16:32, :], send_hbm.at[:, 16:32, :], sems.at[7]),
    ])
    copies[5].wait()
    operators = m2m_ref[...].reshape(2048, 256)
    children = jnp.concatenate([every_eighth(leaf_s, c, 32) for c in range(8)], axis=1)
    parents = dot(children.astype(BF16), operators).astype(BF16)
    parents_ref[...] = parents
    stores += fetch([pltpu.make_async_copy(parents_ref, parents_hbm, sems.at[8])])
    for half in range(2):
        parents_s[half, 0:32, :] = parents[:, 128 * half : 128 * half + 128].astype(F32)
    children = jnp.concatenate([every_eighth(parents_s, c, 8) for c in range(8)], axis=1)
    top = dot(children.astype(BF16), operators)
    for p in range(16):
        send_ref[p, 0:16, :] = jnp.concatenate([sent[8 * p : 8 * p + 8], top], axis=0).astype(BF16)
    stores += fetch([pltpu.make_async_copy(send_ref.at[:, 0:16, :], send_hbm.at[:, 0:16, :], sems.at[9])])
    for copy in stores:
        copy.wait()


def pack(leaf, m2m, rows, count, points, charges):
    return pl.pallas_call(
        pack_kernel,
        out_shape=(
            jax.ShapeDtypeStruct((16, 32, 256), BF16),
            jax.ShapeDtypeStruct((32, 256), BF16),
            jax.ShapeDtypeStruct((4, 8, 128), F32),
        ),
        in_specs=[pl.BlockSpec(memory_space=pltpu.HBM)] * 6,
        out_specs=[pl.BlockSpec(memory_space=pltpu.HBM)] * 3,
        scratch_shapes=[
            pltpu.VMEM((256, 256), BF16),
            pltpu.VMEM((8, 256, 256), BF16),
            pltpu.VMEM((8, 16), I32),
            pltpu.VMEM((16, 16), I32),
            pltpu.VMEM((3, 8, 128), F32),
            pltpu.VMEM((8, 128), F32),
            pltpu.VMEM((2, 256, 128), F32),
            pltpu.VMEM((2, 64, 128), F32),
            pltpu.VMEM((16, 32, 256), BF16),
            pltpu.VMEM((32, 256), BF16),
            pltpu.VMEM((4, 8, 128), F32),
            pltpu.SemaphoreType.DMA((10,)),
        ],
        compiler_params=pltpu.CompilerParams(vmem_limit_bytes=PACK_VMEM),
        cost_estimate=pl.CostEstimate(flops=200_000_000, bytes_accessed=1_500_000, transcendentals=0),
        name="pack",
    )(leaf, m2m, rows, count, points, charges)


def fields(src_ref, val_ref, lanes, base, rows):
    at = iota((rows, 128), 0)
    even = jnp.zeros((rows, 128), I32)
    odd = jnp.zeros((rows, 128), I32)
    for first, last in ((0, 15), (15, 30), (30, 32)):
        word = jnp.zeros((rows, 128), I32)
        for j in range(first, last):
            hit = at == (src_ref[j : j + 1, lanes] - base)
            word += jnp.where(hit, val_ref[j : j + 1, lanes], 0)
        even += word & 0x0F0F0F0F
        odd += (word >> 4) & 0x0F0F0F0F
    return even, odd


def counts_of(even, odd, k):
    word = odd if k % 2 else even
    return ((word >> (8 * (k // 2))) & 0xFF).astype(F32).astype(BF16)


def field_of(cls):
    return jnp.where(cls >= 0, jnp.left_shift(1, 4 * jnp.maximum(cls, 0)), 0)


def lists_kernel(
    leaf_ref, m2l_ref, before_ref, parents_ref, after_ref, edge_ref, src_hbm, cls_hbm, par_src_hbm, par_cls_hbm, top_src_hbm, top_cls_hbm,
    partial_ref, far_ref, par_ref, top_ref,
    src_t, val_t, low_src, low_val, par_src_ref, par_cls_ref, top_src_ref, top_cls_ref, near_w, far_w, z_ref, small_w, par_z, sems,
):
    me = lax.axis_index("gy")
    device = lax.axis_index("gx") * 16 + me
    pairs = (
        (src_hbm, src_t), (cls_hbm, val_t), (par_src_hbm, par_src_ref), (par_cls_hbm, par_cls_ref),
        (top_src_hbm, top_src_ref), (top_cls_hbm, top_cls_ref),
    )
    copies = fetch([pltpu.make_async_copy(a, b, sems.at[i]) for i, (a, b) in enumerate(pairs)])
    leaf = leaf_ref[...]
    for k in range(8):
        z_ref[256 * k : 256 * k + 256, :] = dot(leaf, m2l_ref[k]).astype(BF16)
    bank = jnp.concatenate([before_ref[...], parents_ref[...], after_ref[...]], axis=0)
    for k in range(8):
        z = dot(bank, m2l_ref[k])
        par_z[128 * k : 128 * k + 128, :] = jnp.concatenate([z, jnp.zeros((32, 256), F32)], axis=0).astype(BF16)
    for copy in copies:
        copy.wait()
    src = src_t[...]
    src_t[...] = jnp.where(src >= 4096, src - (4096 - 256), src - 256 * me)
    val_t[...] = field_of(val_t[...])
    src = par_src_ref[...]
    place = (src // 32 - device + 16) // 16
    src = jnp.where(src >= 0, place * 32 + src % 32, -1)
    none = jnp.full((96, 32), -1, I32)
    src = jnp.concatenate([src, none], axis=0).T
    cls = jnp.concatenate([par_cls_ref[...], none], axis=0).T
    top = top_src_ref[...]
    top = jnp.where(top >= 0, (top // 4) * 8 + top % 4, -1)
    none = jnp.full((32, 32), -1, I32)
    low_src[...] = jnp.concatenate([src[:, 0:32], top, none], axis=1)
    low_val[...] = field_of(jnp.concatenate([cls[:, 0:32], top_cls_ref[...], none], axis=1))

    rows = 64

    def near_block(i, _):
        for half in range(2):
            lanes = slice(128 * half, 128 * half + 128)
            even, odd = fields(src_t, val_t, lanes, i * rows, rows)
            for k in range(8):
                near_w[pl.ds(pl.multiple_of(256 * k + i * rows, rows), rows), lanes] = counts_of(even, odd, k)
        return 0

    def far_block(i, _):
        for half in range(2):
            lanes = slice(128 * half, 128 * half + 128)
            even, odd = fields(src_t, val_t, lanes, 256 + i * rows, rows)
            for k in range(8):
                far_w[pl.ds(pl.multiple_of(128 * k + i * rows, rows), rows), lanes] = counts_of(even, odd, k)
        return 0

    def small_block(i, _):
        even, odd = fields(low_src, low_val, slice(0, 128), i * rows, rows)
        for k in range(8):
            small_w[pl.ds(pl.multiple_of(128 * k + i * rows, rows), rows), :] = counts_of(even, odd, k)
        return 0

    lax.fori_loop(0, 4, near_block, 0)
    lax.fori_loop(0, 2, far_block, 0)
    lax.fori_loop(0, 2, small_block, 0)
    partial_ref[...] = dot_tn(near_w[...], z_ref[...])
    for k in range(8):
        far_ref[:, 128 * k : 128 * k + 128] = far_w[128 * k : 128 * k + 128, :].T
    weights = small_w[...].T
    own = (iota((8, 128), 1) == 32 + 4 * me + iota((8, 128), 0)) & (iota((8, 128), 0) < 4)
    own = dot(own.astype(F32).astype(BF16), weights)
    top_ref[...] = jnp.concatenate([own[:, 128 * k : 128 * k + 128] for k in range(8)], axis=0).astype(BF16)
    par_ref[...] = dot(weights[0:32], par_z[...])


def lists(leaf, m2l, before, parents, after, edge, src, cls, par_src, par_cls, top_src, top_cls):
    vmem = pl.BlockSpec(memory_space=pltpu.VMEM)
    return pl.pallas_call(
        lists_kernel,
        out_shape=(
            jax.ShapeDtypeStruct((256, 256), F32),
            jax.ShapeDtypeStruct((256, 1024), BF16),
            jax.ShapeDtypeStruct((32, 256), F32),
            jax.ShapeDtypeStruct((64, 128), BF16),
        ),
        in_specs=[vmem] * 6 + [pl.BlockSpec(memory_space=pltpu.HBM)] * 6,
        scratch_shapes=[
            pltpu.VMEM((32, 256), I32),
            pltpu.VMEM((32, 256), I32),
            pltpu.VMEM((32, 128), I32),
            pltpu.VMEM((32, 128), I32),
            pltpu.VMEM((32, 32), I32),
            pltpu.VMEM((32, 32), I32),
            pltpu.VMEM((32, 64), I32),
            pltpu.VMEM((32, 64), I32),
            pltpu.VMEM((2048, 256), BF16),
            pltpu.VMEM((1024, 256), BF16),
            pltpu.VMEM((2048, 256), BF16),
            pltpu.VMEM((1024, 128), BF16),
            pltpu.VMEM((1024, 256), BF16),
            pltpu.SemaphoreType.DMA((6,)),
        ],
        compiler_params=pltpu.CompilerParams(vmem_limit_bytes=VMEM_LIMIT),
        cost_estimate=pl.CostEstimate(flops=4_000_000_000, bytes_accessed=2_500_000, transcendentals=0),
        name="lists",
    )(leaf, m2l, before, parents, after, edge, src, cls, par_src, par_cls, top_src, top_cls)


def put_rows(ref, first, count, row, value):
    ref[pl.ds(32 * first + row, count, stride=32), :] = value


def put_source(ref, first, count, xyz):
    split = [pieces(x) for x in xyz]
    for row, kind in enumerate((0, 0, 1, 0, 2, 1)):
        for axis in range(3):
            put_rows(ref, first, count, 3 * row + axis, split[axis][kind])
    norm = xyz[0] * xyz[0] + xyz[1] * xyz[1] + xyz[2] * xyz[2]
    for i, part in enumerate(pieces(norm)):
        put_rows(ref, first, count, 18 + i, jnp.ones((count, 128), F32))
        put_rows(ref, first, count, 21 + i, part)


def put_target(ref, xyz):
    split = [pieces(-2.0 * x) for x in xyz]
    for row, kind in enumerate((0, 1, 0, 2, 0, 1)):
        for axis in range(3):
            put_rows(ref, 0, 8, 3 * row + axis, split[axis][kind])
    norm = xyz[0] * xyz[0] + xyz[1] * xyz[1] + xyz[2] * xyz[2] + SOFTENING * SOFTENING
    for i, part in enumerate(pieces(norm)):
        put_rows(ref, 0, 8, 18 + i, part)
        put_rows(ref, 0, 8, 21 + i, jnp.ones((8, 128), F32))


def clear_rows(ref, tiles):
    for s in range(tiles):
        ref[32 * s + 24 : 32 * s + 32, :] = jnp.zeros((8, 128), F32)


def side_by_side(ref):
    return jnp.concatenate([ref[32 * s : 32 * s + 32, :] for s in range(8)], axis=1).astype(BF16)


def near_sum(list_ref, target_of, sources, places, charges, total_s):
    device = lax.axis_index("gx") * 16 + lax.axis_index("gy")
    number = list_ref[...]
    place = jnp.where(number >= 0, number - (device * 8 - HALO_T), -1)
    weights = []
    for i, s in enumerate(places):
        times = jnp.sum((place == s).astype(F32), axis=1, keepdims=True)
        weights.append(times * charges[i : i + 1, :])
    for t in range(8):
        square = dot_tn(target_of(t), sources)
        total = weights[0][t : t + 1, :] * lax.rsqrt(square[:, 0:128])
        for i in range(1, 8):
            total += weights[i][t : t + 1, :] * lax.rsqrt(square[:, 128 * i : 128 * i + 128])
        total_s[128 * t : 128 * t + 128, :] = total
    ones = jnp.ones((8, 128), BF16)
    row = 0.0
    for part in pieces(total_s[...]):
        row += dot_nt(ones, part.astype(BF16))[0:1, :]
    return jnp.concatenate([row[:, 128 * t : 128 * t + 128] for t in range(8)], axis=0)


def own_kernel(
    after_ref, list_ref, points_ref, charges_ref, out_ref, target_ref, source_s, target_s, total_s
):
    xyz = [points_ref[axis] for axis in range(3)]
    clear_rows(source_s, 8)
    clear_rows(target_s, 8)
    put_source(source_s, 0, 8, xyz)
    put_target(target_s, xyz)
    for t in range(8):
        target_ref[t] = target_s[32 * t : 32 * t + 32, :].astype(BF16)
    own = range(HALO_T, HALO_T + 8)
    out_ref[...] = near_sum(
        list_ref, lambda t: target_ref[t], side_by_side(source_s), own, charges_ref[...], total_s
    )


def own_tiles(after, near_src, points, charges):
    return pl.pallas_call(
        own_kernel,
        out_shape=(
            jax.ShapeDtypeStruct((8, 128), F32),
            jax.ShapeDtypeStruct((8, 32, 128), BF16),
        ),
        scratch_shapes=[
            pltpu.VMEM((256, 128), F32),
            pltpu.VMEM((256, 128), F32),
            pltpu.VMEM((1024, 128), F32),
        ],
        compiler_params=pltpu.CompilerParams(vmem_limit_bytes=VMEM_LIMIT),
        cost_estimate=pl.CostEstimate(flops=2_000_000_000, bytes_accessed=100_000, transcendentals=1_000_000),
        name="own_tiles",
    )(after, near_src, points, charges)


def finish_kernel(
    list_ref, target_ref, near_ref, recv_ref, edge_ref, partial_ref, far_ref, par_ref, top_ref, m2l_ref, l2l_ref,
    local_ref, near_out_ref, source_s, total_s, far_z, parents_s, leaves_s,
):
    me = lax.axis_index("gy")
    rows = recv_ref[:, 0:16, :].astype(F32)
    leaf_rows = rows[:, 0:8].reshape(128, 256).astype(BF16)
    top_rows = rows[:, 8:16].reshape(128, 256).astype(BF16)
    buckets = dot(top_ref[...], top_rows).astype(BF16).astype(F32)
    buckets = jnp.concatenate([buckets[8 * k : 8 * k + 8] for k in range(8)], axis=1)
    top_local = dot(buckets.astype(BF16), m2l_ref[...].reshape(2048, 256)).astype(BF16)
    for c in range(8):
        put_every_eighth(parents_s, c, 4, dot(top_local, l2l_ref[c])[0:4])
    for k in range(8):
        far_z[128 * k : 128 * k + 128, :] = dot(leaf_rows, m2l_ref[k]).astype(BF16)
    parent_local = (par_ref[...] + wide(parents_s[...])).astype(BF16)
    for c in range(8):
        put_every_eighth(leaves_s, c, 32, dot(parent_local, l2l_ref[c]))
    total = partial_ref[...] + dot(far_ref[...], far_z[...])
    local_ref[...] = (total + wide(leaves_s[...])).astype(BF16)

    below = recv_ref[jnp.maximum(me - 1, 0), 16:32, :].astype(F32)
    above = recv_ref[jnp.minimum(me + 1, 15), 16:32, :].astype(F32)
    clear_rows(source_s, 8)
    charges = []
    for first, rows, start, end in ((0, below, 4, me == 0), (4, above, 0, me == 15)):
        rows = rows[:, 0:128] + rows[:, 128:256]
        xyzq = [
            jnp.where(end, edge_ref[axis, start : start + 4, :], rows[4 * axis : 4 * axis + 4]) for axis in range(4)
        ]
        put_source(source_s, first, 4, xyzq[0:3])
        charges.append(xyzq[3])
    halo = (0, 1, 2, 3, 12, 13, 14, 15)
    near_out_ref[...] = near_ref[...] + near_sum(
        list_ref, lambda t: target_ref[t], side_by_side(source_s), halo, jnp.concatenate(charges, axis=0), total_s
    )


def finish(near_src, targets, near, recv, edge, partial, far, par, top, m2l, l2l):
    return pl.pallas_call(
        finish_kernel,
        out_shape=(jax.ShapeDtypeStruct((256, 256), BF16), jax.ShapeDtypeStruct((8, 128), F32)),
        scratch_shapes=[
            pltpu.VMEM((256, 128), F32),
            pltpu.VMEM((1024, 128), F32),
            pltpu.VMEM((1024, 256), BF16),
            pltpu.VMEM((2, 32, 128), F32),
            pltpu.VMEM((2, 256, 128), F32),
        ],
        compiler_params=pltpu.CompilerParams(vmem_limit_bytes=VMEM_LIMIT),
        cost_estimate=pl.CostEstimate(flops=3_000_000_000, bytes_accessed=3_500_000, transcendentals=1_000_000),
        name="finish",
    )(near_src, targets, near, recv, edge, partial, far, par, top, m2l, l2l)


def shifted(block, axis, distance):
    size = lax.axis_size(axis)
    route = [(i, i + distance) for i in range(size) if 0 <= i + distance < size]
    return lax.ppermute(block, axis, route)


def across(block):
    rows, width = lax.axis_size("gx"), lax.axis_size("gy")
    ends = [(g * width + width - 1, (g + 1) * width) for g in range(rows - 1)]
    return lax.ppermute(block, ("gx", "gy"), ends + [(b, a) for a, b in ends])


def per_device(
    leaf_moments, leaf_src, leaf_cls, send_rows, send_count, par_src, par_cls, top_src, top_cls,
    points, charges, near_src, m2m_ops, m2l_ops, l2l_ops,
):
    points = points.transpose(1, 0, 2)
    sent, parents, edge = pack(
        leaf_moments, m2m_ops, send_rows[0].transpose(0, 2, 1), send_count[0], points, charges
    )
    edge = across(edge)
    before = shifted(parents, "gx", 1)
    after = shifted(parents, "gx", -1)
    recv = lax.all_to_all(sent, "gy", 0, 0, tiled=True)
    partial, far, par, top = lists(
        leaf_moments, m2l_ops, before, parents, after, edge,
        leaf_src.T, leaf_cls.T, par_src, par_cls, top_src.T, top_cls.T,
    )
    near_own, targets = own_tiles(par, near_src, points, charges)
    return finish(near_src, targets, near_own, recv, edge, partial, far, par, top, m2l_ops, l2l_ops)


def solution(mesh):
    both = P(("gx", "gy"))
    return jax.shard_map(
        per_device,
        mesh=mesh,
        in_specs=(both, both, both, P("gx"), P("gx"), both, both, P("gx"), P("gx"), both, both, both, P(), P(), P()),
        out_specs=(both, both),
        check_vma=False,
    )
```

```python
import jax
import jax.numpy as jnp
from jax import lax
from jax.experimental import pallas as pl
from jax.experimental.pallas import tpu as pltpu
from jax.sharding import PartitionSpec as P

F32 = jnp.float32
BF16 = jnp.bfloat16
I32 = jnp.int32

HALO_T = 4
SOFTENING = 0.05
VMEM_LIMIT = 10 * 1024 * 1024
PACK_VMEM = 10 * 1024 * 1024


def iota(shape, dim):
    return lax.broadcasted_iota(I32, shape, dim)


def dot(a, b):
    return jnp.dot(a, b, preferred_element_type=F32)


def dot_nt(a, b):
    return lax.dot_general(a, b, (((1,), (1,)), ((), ())), preferred_element_type=F32)


def dot_tn(a, b):
    return lax.dot_general(a, b, (((0,), (0,)), ((), ())), preferred_element_type=F32)


def pieces(x):
    high = x.astype(BF16).astype(F32)
    rest = x - high
    middle = rest.astype(BF16).astype(F32)
    return high, middle, rest - middle


def wide(value):
    return jnp.concatenate([value[0], value[1]], axis=1)


def every_eighth(ref, first, count):
    return wide([ref[half, pl.ds(first, count, stride=8), :] for half in range(2)])


def put_every_eighth(ref, first, count, value):
    for half in range(2):
        ref[half, pl.ds(first, count, stride=8), :] = value[:, 128 * half : 128 * half + 128]


def fetch(copies):
    for copy in copies:
        copy.start()
    return copies


def tile_rows(parts, first):
    high = jnp.concatenate([part[0][first : first + HALO_T] for part in parts], axis=0)
    rest = jnp.concatenate([part[1][first : first + HALO_T] for part in parts], axis=0)
    return jnp.concatenate([high, rest], axis=1)


def pack_kernel(
    leaf_hbm, m2m_hbm, rows_hbm, count_hbm, points_hbm, charges_hbm, send_ref, parents_ref, edge_ref,
    leaf_ref, m2m_ref, rows_ref, count_ref, points_ref, charges_ref, leaf_s, parents_s, sems,
):
    me = lax.axis_index("gy")
    pairs = (
        (leaf_hbm, leaf_ref), (rows_hbm.at[me], rows_ref), (count_hbm, count_ref),
        (points_hbm, points_ref), (charges_hbm, charges_ref), (m2m_hbm, m2m_ref),
    )
    copies = fetch([pltpu.make_async_copy(a, b, sems.at[i]) for i, (a, b) in enumerate(pairs)])
    parents_s[:, 32:64, :] = jnp.zeros((2, 32, 128), F32)
    for copy in copies[:5]:
        copy.wait()
    leaf = leaf_ref[...]
    for half in range(2):
        leaf_s[half] = leaf[:, 128 * half : 128 * half + 128].astype(F32)
    table = rows_ref[...].astype(F32)
    live = iota((8, 16), 0) < count_ref[pl.ds(me, 1), :]
    table = jnp.where(live, table, -1.0).astype(BF16)
    repeat = (iota((128, 16), 0) // 8 == iota((128, 16), 1)).astype(F32).astype(BF16)
    spread = dot_nt(repeat, table)
    column = jnp.sum(
        jnp.where(iota((128, 8), 0) % 8 == iota((128, 8), 1), spread, 0.0), axis=1, keepdims=True
    )
    pick = (iota((128, 256), 1).astype(F32) == column).astype(F32).astype(BF16)
    sent = dot(pick, leaf)
    parts = [pieces(x) for x in (points_ref[0], points_ref[1], points_ref[2], charges_ref[...])]
    edge_ref[0:3] = points_ref[...]
    edge_ref[3] = charges_ref[...]
    first = tile_rows(parts, 0)
    last = tile_rows(parts, 8 - HALO_T)
    for p in range(16):
        tiles = jnp.where(me + 1 == p, last, jnp.where(me - 1 == p, first, 0.0))
        send_ref[p, 16:32, :] = tiles.astype(BF16)
    copies[5].wait()
    operators = m2m_ref[...].reshape(2048, 256)
    children = jnp.concatenate([every_eighth(leaf_s, c, 32) for c in range(8)], axis=1)
    parents = dot(children.astype(BF16), operators).astype(BF16)
    parents_ref[...] = parents
    for half in range(2):
        parents_s[half, 0:32, :] = parents[:, 128 * half : 128 * half + 128].astype(F32)
    children = jnp.concatenate([every_eighth(parents_s, c, 8) for c in range(8)], axis=1)
    top = dot(children.astype(BF16), operators)
    for p in range(16):
        send_ref[p, 0:16, :] = jnp.concatenate([sent[8 * p : 8 * p + 8], top], axis=0).astype(BF16)


def pack(leaf, m2m, rows, count, points, charges):
    return pl.pallas_call(
        pack_kernel,
        out_shape=(
            jax.ShapeDtypeStruct((16, 32, 256), BF16),
            jax.ShapeDtypeStruct((32, 256), BF16),
            jax.ShapeDtypeStruct((4, 8, 128), F32),
        ),
        in_specs=[pl.BlockSpec(memory_space=pltpu.HBM)] * 6,
        scratch_shapes=[
            pltpu.VMEM((256, 256), BF16),
            pltpu.VMEM((8, 256, 256), BF16),
            pltpu.VMEM((8, 16), I32),
            pltpu.VMEM((16, 16), I32),
            pltpu.VMEM((3, 8, 128), F32),
            pltpu.VMEM((8, 128), F32),
            pltpu.VMEM((2, 256, 128), F32),
            pltpu.VMEM((2, 64, 128), F32),
            pltpu.SemaphoreType.DMA((6,)),
        ],
        compiler_params=pltpu.CompilerParams(vmem_limit_bytes=PACK_VMEM),
        cost_estimate=pl.CostEstimate(flops=200_000_000, bytes_accessed=1_500_000, transcendentals=0),
        name="pack",
    )(*[pltpu.with_memory_space_constraint(x, pltpu.HBM) for x in (leaf, m2m, rows, count, points, charges)])


def fields(src_ref, val_ref, lanes, base, rows):
    at = iota((rows, 128), 0)
    even = jnp.zeros((rows, 128), I32)
    odd = jnp.zeros((rows, 128), I32)
    for first, last in ((0, 15), (15, 30), (30, 32)):
        word = jnp.zeros((rows, 128), I32)
        for j in range(first, last):
            hit = at == (src_ref[j : j + 1, lanes] - base)
            word += jnp.where(hit, val_ref[j : j + 1, lanes], 0)
        even += word & 0x0F0F0F0F
        odd += (word >> 4) & 0x0F0F0F0F
    return even, odd


def counts_of(even, odd, k):
    word = odd if k % 2 else even
    return ((word >> (8 * (k // 2))) & 0xFF).astype(F32).astype(BF16)


def field_of(cls):
    return jnp.where(cls >= 0, jnp.left_shift(1, 4 * jnp.maximum(cls, 0)), 0)


def lists_kernel(
    leaf_ref, m2l_ref, parents_ref, edge_ref, src_hbm, cls_hbm, par_src_hbm, par_cls_hbm, top_src_hbm, top_cls_hbm,
    partial_ref, far_ref, par_ref, top_ref, parents_out,
    src_t, val_t, low_src, low_val, par_src_ref, par_cls_ref, top_src_ref, top_cls_ref, near_w, far_w, z_ref, small_w, sems,
):
    me = lax.axis_index("gy")
    device = lax.axis_index("gx") * 16 + me
    pairs = (
        (src_hbm, src_t), (cls_hbm, val_t), (par_src_hbm, par_src_ref), (par_cls_hbm, par_cls_ref),
        (top_src_hbm, top_src_ref), (top_cls_hbm, top_cls_ref),
    )
    copies = fetch([pltpu.make_async_copy(a, b, sems.at[i]) for i, (a, b) in enumerate(pairs)])
    leaf = leaf_ref[...]
    for k in range(8):
        z_ref[256 * k : 256 * k + 256, :] = dot(leaf, m2l_ref[k]).astype(BF16)
    parents_out[...] = parents_ref[...]
    for copy in copies:
        copy.wait()
    src = src_t[...]
    src_t[...] = jnp.where(src >= 4096, src - (4096 - 256), src - 256 * me)
    val_t[...] = field_of(val_t[...])
    src = par_src_ref[...]
    place = (src // 32 - device + 16) // 16
    src = jnp.where(src >= 0, place * 32 + src % 32, -1)
    none = jnp.full((96, 32), -1, I32)
    src = jnp.concatenate([src, none], axis=0).T
    cls = jnp.concatenate([par_cls_ref[...], none], axis=0).T
    top = top_src_ref[...]
    top = jnp.where(top >= 0, (top // 4) * 8 + top % 4, -1)
    none = jnp.full((32, 32), -1, I32)
    low_src[...] = jnp.concatenate([src[:, 0:32], top, none], axis=1)
    low_val[...] = field_of(jnp.concatenate([cls[:, 0:32], top_cls_ref[...], none], axis=1))

    rows = 64

    def near_block(i, _):
        for half in range(2):
            lanes = slice(128 * half, 128 * half + 128)
            even, odd = fields(src_t, val_t, lanes, i * rows, rows)
            for k in range(8):
                near_w[pl.ds(pl.multiple_of(256 * k + i * rows, rows), rows), lanes] = counts_of(even, odd, k)
        return 0

    def far_block(i, _):
        for half in range(2):
            lanes = slice(128 * half, 128 * half + 128)
            even, odd = fields(src_t, val_t, lanes, 256 + i * rows, rows)
            for k in range(8):
                far_w[pl.ds(pl.multiple_of(128 * k + i * rows, rows), rows), lanes] = counts_of(even, odd, k)
        return 0

    def small_block(i, _):
        even, odd = fields(low_src, low_val, slice(0, 128), i * rows, rows)
        for k in range(8):
            small_w[pl.ds(pl.multiple_of(128 * k + i * rows, rows), rows), :] = counts_of(even, odd, k)
        return 0

    lax.fori_loop(0, 4, near_block, 0)
    lax.fori_loop(0, 2, far_block, 0)
    lax.fori_loop(0, 2, small_block, 0)
    partial_ref[...] = dot_tn(near_w[...], z_ref[...])
    for k in range(8):
        far_ref[:, 128 * k : 128 * k + 128] = far_w[128 * k : 128 * k + 128, :].T
    weights = small_w[...].T
    own = (iota((8, 128), 1) == 32 + 4 * me + iota((8, 128), 0)) & (iota((8, 128), 0) < 4)
    own = dot(own.astype(F32).astype(BF16), weights)
    top_ref[...] = jnp.concatenate([own[:, 128 * k : 128 * k + 128] for k in range(8)], axis=0).astype(BF16)
    for k in range(8):
        par_ref[32 * k : 32 * k + 32, :] = weights[0:32, 128 * k : 128 * k + 128]


def lists(leaf, m2l, parents, edge, src, cls, par_src, par_cls, top_src, top_cls):
    vmem = pl.BlockSpec(memory_space=pltpu.VMEM)
    return pl.pallas_call(
        lists_kernel,
        out_shape=(
            jax.ShapeDtypeStruct((256, 256), F32),
            jax.ShapeDtypeStruct((256, 1024), BF16),
            jax.ShapeDtypeStruct((256, 128), BF16),
            jax.ShapeDtypeStruct((64, 128), BF16),
            jax.ShapeDtypeStruct((32, 256), BF16),
        ),
        in_specs=[vmem] * 4 + [pl.BlockSpec(memory_space=pltpu.HBM)] * 6,
        scratch_shapes=[
            pltpu.VMEM((32, 256), I32),
            pltpu.VMEM((32, 256), I32),
            pltpu.VMEM((32, 128), I32),
            pltpu.VMEM((32, 128), I32),
            pltpu.VMEM((32, 32), I32),
            pltpu.VMEM((32, 32), I32),
            pltpu.VMEM((32, 64), I32),
            pltpu.VMEM((32, 64), I32),
            pltpu.VMEM((2048, 256), BF16),
            pltpu.VMEM((1024, 256), BF16),
            pltpu.VMEM((2048, 256), BF16),
            pltpu.VMEM((1024, 128), BF16),
            pltpu.SemaphoreType.DMA((6,)),
        ],
        compiler_params=pltpu.CompilerParams(vmem_limit_bytes=VMEM_LIMIT),
        cost_estimate=pl.CostEstimate(flops=4_000_000_000, bytes_accessed=2_500_000, transcendentals=0),
        name="lists",
    )(leaf, m2l, parents, edge, src, cls, par_src, par_cls, top_src, top_cls)


def put_rows(ref, first, count, row, value):
    ref[pl.ds(32 * first + row, count, stride=32), :] = value


def put_source(ref, first, count, xyz):
    split = [pieces(x) for x in xyz]
    for row, kind in enumerate((0, 0, 1, 0, 2, 1)):
        for axis in range(3):
            put_rows(ref, first, count, 3 * row + axis, split[axis][kind])
    norm = xyz[0] * xyz[0] + xyz[1] * xyz[1] + xyz[2] * xyz[2]
    for i, part in enumerate(pieces(norm)):
        put_rows(ref, first, count, 18 + i, jnp.ones((count, 128), F32))
        put_rows(ref, first, count, 21 + i, part)


def put_target(ref, xyz):
    split = [pieces(-2.0 * x) for x in xyz]
    for row, kind in enumerate((0, 1, 0, 2, 0, 1)):
        for axis in range(3):
            put_rows(ref, 0, 8, 3 * row + axis, split[axis][kind])
    norm = xyz[0] * xyz[0] + xyz[1] * xyz[1] + xyz[2] * xyz[2] + SOFTENING * SOFTENING
    for i, part in enumerate(pieces(norm)):
        put_rows(ref, 0, 8, 18 + i, part)
        put_rows(ref, 0, 8, 21 + i, jnp.ones((8, 128), F32))


def clear_rows(ref, tiles):
    for s in range(tiles):
        ref[32 * s + 24 : 32 * s + 32, :] = jnp.zeros((8, 128), F32)


def side_by_side(ref):
    return jnp.concatenate([ref[32 * s : 32 * s + 32, :] for s in range(8)], axis=1).astype(BF16)


def near_sum(list_ref, target_of, sources, places, charges, total_s):
    device = lax.axis_index("gx") * 16 + lax.axis_index("gy")
    number = list_ref[...]
    place = jnp.where(number >= 0, number - (device * 8 - HALO_T), -1)
    weights = []
    for i, s in enumerate(places):
        times = jnp.sum((place == s).astype(F32), axis=1, keepdims=True)
        weights.append(times * charges[i : i + 1, :])
    for t in range(8):
        square = dot_tn(target_of(t), sources)
        total = weights[0][t : t + 1, :] * lax.rsqrt(square[:, 0:128])
        for i in range(1, 8):
            total += weights[i][t : t + 1, :] * lax.rsqrt(square[:, 128 * i : 128 * i + 128])
        total_s[128 * t : 128 * t + 128, :] = total
    ones = jnp.ones((8, 128), BF16)
    row = 0.0
    for part in pieces(total_s[...]):
        row += dot_nt(ones, part.astype(BF16))[0:1, :]
    return jnp.concatenate([row[:, 128 * t : 128 * t + 128] for t in range(8)], axis=0)


def own_kernel(
    after_ref, list_ref, points_ref, charges_ref, out_ref, target_ref, source_s, target_s, total_s
):
    xyz = [points_ref[axis] for axis in range(3)]
    clear_rows(source_s, 8)
    clear_rows(target_s, 8)
    put_source(source_s, 0, 8, xyz)
    put_target(target_s, xyz)
    for t in range(8):
        target_ref[t] = target_s[32 * t : 32 * t + 32, :].astype(BF16)
    own = range(HALO_T, HALO_T + 8)
    out_ref[...] = near_sum(
        list_ref, lambda t: target_ref[t], side_by_side(source_s), own, charges_ref[...], total_s
    )


def own_tiles(after, near_src, points, charges):
    return pl.pallas_call(
        own_kernel,
        out_shape=(
            jax.ShapeDtypeStruct((8, 128), F32),
            jax.ShapeDtypeStruct((8, 32, 128), BF16),
        ),
        scratch_shapes=[
            pltpu.VMEM((256, 128), F32),
            pltpu.VMEM((256, 128), F32),
            pltpu.VMEM((1024, 128), F32),
        ],
        compiler_params=pltpu.CompilerParams(vmem_limit_bytes=VMEM_LIMIT),
        cost_estimate=pl.CostEstimate(flops=2_000_000_000, bytes_accessed=100_000, transcendentals=1_000_000),
        name="own_tiles",
    )(after, near_src, points, charges)


def finish_kernel(
    list_ref, target_ref, near_ref, recv_ref, edge_ref, partial_ref, far_ref, top_ref, m2l_ref, l2l_ref,
    field_ref, from_top_ref, near_out_ref, source_s, total_s, far_z, parents_s,
):
    me = lax.axis_index("gy")
    rows = recv_ref[:, 0:16, :].astype(F32)
    leaf_rows = rows[:, 0:8].reshape(128, 256).astype(BF16)
    top_rows = rows[:, 8:16].reshape(128, 256).astype(BF16)
    buckets = dot(top_ref[...], top_rows).astype(BF16).astype(F32)
    buckets = jnp.concatenate([buckets[8 * k : 8 * k + 8] for k in range(8)], axis=1)
    top_local = dot(buckets.astype(BF16), m2l_ref[...].reshape(2048, 256)).astype(BF16)
    for c in range(8):
        put_every_eighth(parents_s, c, 4, dot(top_local, l2l_ref[c])[0:4])
    for k in range(8):
        far_z[128 * k : 128 * k + 128, :] = dot(leaf_rows, m2l_ref[k]).astype(BF16)
    from_top_ref[...] = wide(parents_s[...])
    field_ref[...] = partial_ref[...] + dot(far_ref[...], far_z[...])

    below = recv_ref[jnp.maximum(me - 1, 0), 16:32, :].astype(F32)
    above = recv_ref[jnp.minimum(me + 1, 15), 16:32, :].astype(F32)
    clear_rows(source_s, 8)
    charges = []
    for first, rows, start, end in ((0, below, 4, me == 0), (4, above, 0, me == 15)):
        rows = rows[:, 0:128] + rows[:, 128:256]
        xyzq = [
            jnp.where(end, edge_ref[axis, start : start + 4, :], rows[4 * axis : 4 * axis + 4]) for axis in range(4)
        ]
        put_source(source_s, first, 4, xyzq[0:3])
        charges.append(xyzq[3])
    halo = (0, 1, 2, 3, 12, 13, 14, 15)
    near_out_ref[...] = near_ref[...] + near_sum(
        list_ref, lambda t: target_ref[t], side_by_side(source_s), halo, jnp.concatenate(charges, axis=0), total_s
    )


def finish(near_src, targets, near, recv, edge, partial, far, top, m2l, l2l):
    return pl.pallas_call(
        finish_kernel,
        out_shape=(
            jax.ShapeDtypeStruct((256, 256), F32),
            jax.ShapeDtypeStruct((32, 256), F32),
            jax.ShapeDtypeStruct((8, 128), F32),
        ),
        scratch_shapes=[
            pltpu.VMEM((256, 128), F32),
            pltpu.VMEM((1024, 128), F32),
            pltpu.VMEM((1024, 256), BF16),
            pltpu.VMEM((2, 32, 128), F32),
        ],
        compiler_params=pltpu.CompilerParams(vmem_limit_bytes=VMEM_LIMIT),
        cost_estimate=pl.CostEstimate(flops=3_000_000_000, bytes_accessed=3_500_000, transcendentals=1_000_000),
        name="finish",
    )(near_src, targets, near, recv, edge, partial, far, top, m2l, l2l)


def leaves_kernel(
    before_ref, parents_ref, after_ref, par_ref, from_top_ref, field_ref, m2l_ref, l2l_ref, local_ref, leaves_s
):
    bank = jnp.concatenate(
        [before_ref[...], parents_ref[...], after_ref[...], jnp.zeros((32, 256), BF16)], axis=0
    )
    buckets = dot(par_ref[...], bank).astype(BF16)
    buckets = jnp.concatenate([buckets[32 * k : 32 * k + 32] for k in range(8)], axis=1)
    field = dot(buckets, m2l_ref[...].reshape(2048, 256))
    parent_local = (field + from_top_ref[...]).astype(BF16)
    for c in range(8):
        put_every_eighth(leaves_s, c, 32, dot(parent_local, l2l_ref[c]))
    local_ref[...] = (field_ref[...] + wide(leaves_s[...])).astype(BF16)


def leaves(before, parents, after, par, from_top, field, m2l, l2l):
    return pl.pallas_call(
        leaves_kernel,
        out_shape=jax.ShapeDtypeStruct((256, 256), BF16),
        scratch_shapes=[pltpu.VMEM((2, 256, 128), F32)],
        compiler_params=pltpu.CompilerParams(vmem_limit_bytes=VMEM_LIMIT),
        cost_estimate=pl.CostEstimate(flops=500_000_000, bytes_accessed=3_000_000, transcendentals=0),
        name="leaves",
    )(before, parents, after, par, from_top, field, m2l, l2l)


def shifted(block, axis, distance):
    size = lax.axis_size(axis)
    route = [(i, i + distance) for i in range(size) if 0 <= i + distance < size]
    return lax.ppermute(block, axis, route)


def across(block):
    rows, width = lax.axis_size("gx"), lax.axis_size("gy")
    ends = [(g * width + width - 1, (g + 1) * width) for g in range(rows - 1)]
    return lax.ppermute(block, ("gx", "gy"), ends + [(b, a) for a, b in ends])


def per_device(
    leaf_moments, leaf_src, leaf_cls, send_rows, send_count, par_src, par_cls, top_src, top_cls,
    points, charges, near_src, m2m_ops, m2l_ops, l2l_ops,
):
    points = points.transpose(1, 0, 2)
    sent, parents, edge = pack(
        leaf_moments, m2m_ops, send_rows[0].transpose(0, 2, 1), send_count[0], points, charges
    )
    edge = across(edge)
    recv = lax.all_to_all(sent, "gy", 0, 0, tiled=True)
    partial, far, par, top, parents = lists(
        leaf_moments, m2l_ops, parents, edge,
        leaf_src.T, leaf_cls.T, par_src, par_cls, top_src.T, top_cls.T,
    )
    before = shifted(parents, "gx", 1)
    after = shifted(parents, "gx", -1)
    near_own, targets = own_tiles(top, near_src, points, charges)
    field, from_top, near_total = finish(
        near_src, targets, near_own, recv, edge, partial, far, top, m2l_ops, l2l_ops
    )
    leaf_local = leaves(before, parents, after, par, from_top, field, m2l_ops, l2l_ops)
    return leaf_local, near_total


def solution(mesh):
    both = P(("gx", "gy"))
    return jax.shard_map(
        per_device,
        mesh=mesh,
        in_specs=(both, both, both, P("gx"), P("gx"), both, both, P("gx"), P("gx"), both, both, both, P(), P(), P()),
        out_specs=(both, both),
        check_vma=False,
    )
```

```python
import jax
import jax.numpy as jnp
from jax import lax
from jax.experimental import pallas as pl
from jax.experimental.pallas import tpu as pltpu
from jax.sharding import PartitionSpec as P

F32 = jnp.float32
BF16 = jnp.bfloat16
I32 = jnp.int32

HALO_T = 4
SOFTENING = 0.05
VMEM_LIMIT = 10 * 1024 * 1024


def iota(shape, dim):
    return lax.broadcasted_iota(I32, shape, dim)


def dot(a, b):
    return jnp.dot(a, b, preferred_element_type=F32)


def dot_nt(a, b):
    return lax.dot_general(a, b, (((1,), (1,)), ((), ())), preferred_element_type=F32)


def dot_tn(a, b):
    return lax.dot_general(a, b, (((0,), (0,)), ((), ())), preferred_element_type=F32)


def pieces(x):
    high = x.astype(BF16).astype(F32)
    rest = x - high
    middle = rest.astype(BF16).astype(F32)
    return high, middle, rest - middle


def wide(value):
    return jnp.concatenate([value[0], value[1]], axis=1)


def every_eighth(ref, first, count):
    return wide([ref[half, pl.ds(first, count, stride=8), :] for half in range(2)])


def put_every_eighth(ref, first, count, value):
    for half in range(2):
        ref[half, pl.ds(first, count, stride=8), :] = value[:, 128 * half : 128 * half + 128]


def fetch(copies):
    for copy in copies:
        copy.start()
    return copies


def tile_rows(parts, first):
    high = jnp.concatenate([part[0][first : first + HALO_T] for part in parts], axis=0)
    rest = jnp.concatenate([part[1][first : first + HALO_T] for part in parts], axis=0)
    return jnp.concatenate([high, rest], axis=1)


def pack_kernel(
    leaf_hbm, m2m_hbm, rows_hbm, count_hbm, points_hbm, charges_hbm, send_ref, up_ref, down_ref,
    leaf_ref, m2m_ref, rows_ref, count_ref, points_ref, charges_ref, leaf_s, parents_s, sems,
):
    me = lax.axis_index("gy")
    pairs = (
        (leaf_hbm, leaf_ref), (rows_hbm.at[me], rows_ref), (count_hbm, count_ref),
        (points_hbm, points_ref), (charges_hbm, charges_ref), (m2m_hbm, m2m_ref),
    )
    copies = fetch([pltpu.make_async_copy(a, b, sems.at[i]) for i, (a, b) in enumerate(pairs)])
    parents_s[:, 32:64, :] = jnp.zeros((2, 32, 128), F32)
    for copy in copies[:5]:
        copy.wait()
    leaf = leaf_ref[...]
    for half in range(2):
        leaf_s[half] = leaf[:, 128 * half : 128 * half + 128].astype(F32)
    table = rows_ref[...].astype(F32)
    live = iota((8, 16), 0) < count_ref[pl.ds(me, 1), :]
    table = jnp.where(live, table, -1.0).astype(BF16)
    repeat = (iota((128, 16), 0) // 8 == iota((128, 16), 1)).astype(F32).astype(BF16)
    spread = dot_nt(repeat, table)
    column = jnp.sum(
        jnp.where(iota((128, 8), 0) % 8 == iota((128, 8), 1), spread, 0.0), axis=1, keepdims=True
    )
    pick = (iota((128, 256), 1).astype(F32) == column).astype(F32).astype(BF16)
    sent = dot(pick, leaf)
    parts = [pieces(x) for x in (points_ref[0], points_ref[1], points_ref[2], charges_ref[...])]
    first = tile_rows(parts, 0)
    last = tile_rows(parts, 8 - HALO_T)
    for p in range(16):
        tiles = jnp.where(me + 1 == p, last, jnp.where(me - 1 == p, first, 0.0))
        send_ref[p, 16:32, :] = tiles.astype(BF16)
    up_ref[32:48, :] = last.astype(BF16)
    down_ref[32:48, :] = first.astype(BF16)
    copies[5].wait()
    operators = m2m_ref[...].reshape(2048, 256)
    children = jnp.concatenate([every_eighth(leaf_s, c, 32) for c in range(8)], axis=1)
    parents = dot(children.astype(BF16), operators).astype(BF16)
    up_ref[0:32, :] = parents
    down_ref[0:32, :] = parents
    for half in range(2):
        parents_s[half, 0:32, :] = parents[:, 128 * half : 128 * half + 128].astype(F32)
    children = jnp.concatenate([every_eighth(parents_s, c, 8) for c in range(8)], axis=1)
    top = dot(children.astype(BF16), operators)
    for p in range(16):
        send_ref[p, 0:16, :] = jnp.concatenate([sent[8 * p : 8 * p + 8], top], axis=0).astype(BF16)


def pack(leaf, m2m, rows, count, points, charges):
    return pl.pallas_call(
        pack_kernel,
        out_shape=(
            jax.ShapeDtypeStruct((16, 32, 256), BF16),
            jax.ShapeDtypeStruct((48, 256), BF16),
            jax.ShapeDtypeStruct((48, 256), BF16),
        ),
        in_specs=[pl.BlockSpec(memory_space=pltpu.HBM)] * 6,
        scratch_shapes=[
            pltpu.VMEM((256, 256), BF16),
            pltpu.VMEM((8, 256, 256), BF16),
            pltpu.VMEM((8, 16), I32),
            pltpu.VMEM((16, 16), I32),
            pltpu.VMEM((3, 8, 128), F32),
            pltpu.VMEM((8, 128), F32),
            pltpu.VMEM((2, 256, 128), F32),
            pltpu.VMEM((2, 64, 128), F32),
            pltpu.SemaphoreType.DMA((6,)),
        ],
        compiler_params=pltpu.CompilerParams(vmem_limit_bytes=VMEM_LIMIT),
        cost_estimate=pl.CostEstimate(flops=200_000_000, bytes_accessed=1_500_000, transcendentals=0),
        name="pack",
    )(*[pltpu.with_memory_space_constraint(x, pltpu.HBM) for x in (leaf, m2m, rows, count, points, charges)])


def ends_kernel(send_ref, before_ref, after_ref, out_ref):
    me = lax.axis_index("gy")
    out_ref[...] = send_ref[...]

    @pl.when(me == 15)
    def _():
        out_ref[0, 16:32, :] = before_ref[32:48, :]

    @pl.when(me == 0)
    def _():
        out_ref[15, 16:32, :] = after_ref[32:48, :]


def with_ends(send, before, after):
    return pl.pallas_call(
        ends_kernel,
        out_shape=jax.ShapeDtypeStruct((16, 32, 256), BF16),
        compiler_params=pltpu.CompilerParams(vmem_limit_bytes=VMEM_LIMIT),
        name="with_ends",
    )(send, before, after)


def fields(src_ref, val_ref, lanes, base, rows):
    at = iota((rows, 128), 0)
    even = jnp.zeros((rows, 128), I32)
    odd = jnp.zeros((rows, 128), I32)
    for first, last in ((0, 15), (15, 30), (30, 32)):
        word = jnp.zeros((rows, 128), I32)
        for j in range(first, last):
            hit = at == (src_ref[j : j + 1, lanes] - base)
            word += jnp.where(hit, val_ref[j : j + 1, lanes], 0)
        even += word & 0x0F0F0F0F
        odd += (word >> 4) & 0x0F0F0F0F
    return even, odd


def counts_of(even, odd, k):
    word = odd if k % 2 else even
    return ((word >> (8 * (k // 2))) & 0xFF).astype(F32).astype(BF16)


def field_of(cls):
    return jnp.where(cls >= 0, jnp.left_shift(1, 4 * jnp.maximum(cls, 0)), 0)


def lists_kernel(
    leaf_ref, m2l_ref, before_ref, parents_ref, after_ref, src_hbm, cls_hbm, par_src_hbm, par_cls_hbm, top_src_hbm, top_cls_hbm,
    partial_ref, far_ref, par_ref, top_ref,
    src_t, val_t, low_src, low_val, par_src_ref, par_cls_ref, top_src_ref, top_cls_ref, near_w, far_w, z_ref, small_w, par_z, sems,
):
    me = lax.axis_index("gy")
    device = lax.axis_index("gx") * 16 + me
    pairs = (
        (src_hbm, src_t), (cls_hbm, val_t), (par_src_hbm, par_src_ref), (par_cls_hbm, par_cls_ref),
        (top_src_hbm, top_src_ref), (top_cls_hbm, top_cls_ref),
    )
    copies = fetch([pltpu.make_async_copy(a, b, sems.at[i]) for i, (a, b) in enumerate(pairs)])
    leaf = leaf_ref[...]
    for k in range(8):
        z_ref[256 * k : 256 * k + 256, :] = dot(leaf, m2l_ref[k]).astype(BF16)
    bank = jnp.concatenate([before_ref[0:32, :], parents_ref[0:32, :], after_ref[0:32, :]], axis=0)
    for k in range(8):
        z = dot(bank, m2l_ref[k])
        par_z[128 * k : 128 * k + 128, :] = jnp.concatenate([z, jnp.zeros((32, 256), F32)], axis=0).astype(BF16)
    for copy in copies:
        copy.wait()
    src = src_t[...]
    src_t[...] = jnp.where(src >= 4096, src - (4096 - 256), src - 256 * me)
    val_t[...] = field_of(val_t[...])
    src = par_src_ref[...]
    place = (src // 32 - device + 16) // 16
    src = jnp.where(src >= 0, place * 32 + src % 32, -1)
    none = jnp.full((96, 32), -1, I32)
    src = jnp.concatenate([src, none], axis=0).T
    cls = jnp.concatenate([par_cls_ref[...], none], axis=0).T
    top = top_src_ref[...]
    top = jnp.where(top >= 0, (top // 4) * 8 + top % 4, -1)
    none = jnp.full((32, 32), -1, I32)
    low_src[...] = jnp.concatenate([src[:, 0:32], top, none], axis=1)
    low_val[...] = field_of(jnp.concatenate([cls[:, 0:32], top_cls_ref[...], none], axis=1))

    rows = 64

    def near_block(i, _):
        for half in range(2):
            lanes = slice(128 * half, 128 * half + 128)
            even, odd = fields(src_t, val_t, lanes, i * rows, rows)
            for k in range(8):
                near_w[pl.ds(pl.multiple_of(256 * k + i * rows, rows), rows), lanes] = counts_of(even, odd, k)
        return 0

    def far_block(i, _):
        for half in range(2):
            lanes = slice(128 * half, 128 * half + 128)
            even, odd = fields(src_t, val_t, lanes, 256 + i * rows, rows)
            for k in range(8):
                far_w[pl.ds(pl.multiple_of(128 * k + i * rows, rows), rows), lanes] = counts_of(even, odd, k)
        return 0

    def small_block(i, _):
        even, odd = fields(low_src, low_val, slice(0, 128), i * rows, rows)
        for k in range(8):
            small_w[pl.ds(pl.multiple_of(128 * k + i * rows, rows), rows), :] = counts_of(even, odd, k)
        return 0

    lax.fori_loop(0, 4, near_block, 0)
    lax.fori_loop(0, 2, far_block, 0)
    lax.fori_loop(0, 2, small_block, 0)
    partial_ref[...] = dot_tn(near_w[...], z_ref[...])
    for k in range(8):
        far_ref[:, 128 * k : 128 * k + 128] = far_w[128 * k : 128 * k + 128, :].T
    weights = small_w[...].T
    own = (iota((8, 128), 1) == 32 + 4 * me + iota((8, 128), 0)) & (iota((8, 128), 0) < 4)
    own = dot(own.astype(F32).astype(BF16), weights)
    top_ref[...] = jnp.concatenate([own[:, 128 * k : 128 * k + 128] for k in range(8)], axis=0).astype(BF16)
    par_ref[...] = dot(weights[0:32], par_z[...])


def lists(leaf, m2l, before, parents, after, src, cls, par_src, par_cls, top_src, top_cls):
    vmem = pl.BlockSpec(memory_space=pltpu.VMEM)
    return pl.pallas_call(
        lists_kernel,
        out_shape=(
            jax.ShapeDtypeStruct((256, 256), F32),
            jax.ShapeDtypeStruct((256, 1024), BF16),
            jax.ShapeDtypeStruct((32, 256), F32),
            jax.ShapeDtypeStruct((64, 128), BF16),
        ),
        in_specs=[vmem] * 5 + [pl.BlockSpec(memory_space=pltpu.HBM)] * 6,
        scratch_shapes=[
            pltpu.VMEM((32, 256), I32),
            pltpu.VMEM((32, 256), I32),
            pltpu.VMEM((32, 128), I32),
            pltpu.VMEM((32, 128), I32),
            pltpu.VMEM((32, 32), I32),
            pltpu.VMEM((32, 32), I32),
            pltpu.VMEM((32, 64), I32),
            pltpu.VMEM((32, 64), I32),
            pltpu.VMEM((2048, 256), BF16),
            pltpu.VMEM((1024, 256), BF16),
            pltpu.VMEM((2048, 256), BF16),
            pltpu.VMEM((1024, 128), BF16),
            pltpu.VMEM((1024, 256), BF16),
            pltpu.SemaphoreType.DMA((6,)),
        ],
        compiler_params=pltpu.CompilerParams(vmem_limit_bytes=VMEM_LIMIT),
        cost_estimate=pl.CostEstimate(flops=4_000_000_000, bytes_accessed=2_500_000, transcendentals=0),
        name="lists",
    )(leaf, m2l, before, parents, after, src, cls, par_src, par_cls, top_src, top_cls)


def put_rows(ref, first, count, row, value):
    ref[pl.ds(32 * first + row, count, stride=32), :] = value


def put_source(ref, first, count, xyz):
    split = [pieces(x) for x in xyz]
    for row, kind in enumerate((0, 0, 1, 0, 2, 1)):
        for axis in range(3):
            put_rows(ref, first, count, 3 * row + axis, split[axis][kind])
    norm = xyz[0] * xyz[0] + xyz[1] * xyz[1] + xyz[2] * xyz[2]
    for i, part in enumerate(pieces(norm)):
        put_rows(ref, first, count, 18 + i, jnp.ones((count, 128), F32))
        put_rows(ref, first, count, 21 + i, part)


def put_target(ref, xyz):
    split = [pieces(-2.0 * x) for x in xyz]
    for row, kind in enumerate((0, 1, 0, 2, 0, 1)):
        for axis in range(3):
            put_rows(ref, 0, 8, 3 * row + axis, split[axis][kind])
    norm = xyz[0] * xyz[0] + xyz[1] * xyz[1] + xyz[2] * xyz[2] + SOFTENING * SOFTENING
    for i, part in enumerate(pieces(norm)):
        put_rows(ref, 0, 8, 18 + i, part)
        put_rows(ref, 0, 8, 21 + i, jnp.ones((8, 128), F32))


def clear_rows(ref, tiles):
    for s in range(tiles):
        ref[32 * s + 24 : 32 * s + 32, :] = jnp.zeros((8, 128), F32)


def side_by_side(ref):
    return jnp.concatenate([ref[32 * s : 32 * s + 32, :] for s in range(8)], axis=1).astype(BF16)


def tiles_of(rows):
    rows = rows.astype(F32)
    rows = rows[:, 0:128] + rows[:, 128:256]
    return [rows[4 * i : 4 * i + 4] for i in range(4)]


def near_sum(list_ref, target_of, sources, places, charges, total_s):
    device = lax.axis_index("gx") * 16 + lax.axis_index("gy")
    number = list_ref[...]
    place = jnp.where(number >= 0, number - (device * 8 - HALO_T), -1)
    weights = []
    for i, s in enumerate(places):
        times = jnp.sum((place == s).astype(F32), axis=1, keepdims=True)
        weights.append(times * charges[i : i + 1, :])
    for t in range(8):
        square = dot_tn(target_of(t), sources)
        total = weights[0][t : t + 1, :] * lax.rsqrt(square[:, 0:128])
        for i in range(1, 8):
            total += weights[i][t : t + 1, :] * lax.rsqrt(square[:, 128 * i : 128 * i + 128])
        total_s[128 * t : 128 * t + 128, :] = total
    ones = jnp.ones((8, 128), BF16)
    row = 0.0
    for part in pieces(total_s[...]):
        row += dot_nt(ones, part.astype(BF16))[0:1, :]
    return jnp.concatenate([row[:, 128 * t : 128 * t + 128] for t in range(8)], axis=0)


def own_kernel(
    after_ref, list_ref, points_ref, charges_ref, out_ref, target_ref, source_s, target_s, total_s
):
    xyz = [points_ref[axis] for axis in range(3)]
    clear_rows(source_s, 8)
    clear_rows(target_s, 8)
    put_source(source_s, 0, 8, xyz)
    put_target(target_s, xyz)
    for t in range(8):
        target_ref[t] = target_s[32 * t : 32 * t + 32, :].astype(BF16)
    own = range(HALO_T, HALO_T + 8)
    out_ref[...] = near_sum(
        list_ref, lambda t: target_ref[t], side_by_side(source_s), own, charges_ref[...], total_s
    )


def own_tiles(after, near_src, points, charges):
    return pl.pallas_call(
        own_kernel,
        out_shape=(
            jax.ShapeDtypeStruct((8, 128), F32),
            jax.ShapeDtypeStruct((8, 32, 128), BF16),
        ),
        scratch_shapes=[
            pltpu.VMEM((256, 128), F32),
            pltpu.VMEM((256, 128), F32),
            pltpu.VMEM((1024, 128), F32),
        ],
        compiler_params=pltpu.CompilerParams(vmem_limit_bytes=VMEM_LIMIT),
        cost_estimate=pl.CostEstimate(flops=2_000_000_000, bytes_accessed=100_000, transcendentals=1_000_000),
        name="own_tiles",
    )(after, near_src, points, charges)


def finish_kernel(
    list_ref, target_ref, near_ref, recv_ref, partial_ref, far_ref, par_ref, top_ref, m2l_ref, l2l_ref,
    local_ref, near_out_ref, source_s, total_s, far_z, parents_s, leaves_s,
):
    me = lax.axis_index("gy")
    rows = recv_ref[:, 0:16, :].astype(F32)
    leaf_rows = rows[:, 0:8].reshape(128, 256).astype(BF16)
    top_rows = rows[:, 8:16].reshape(128, 256).astype(BF16)
    buckets = dot(top_ref[...], top_rows).astype(BF16).astype(F32)
    buckets = jnp.concatenate([buckets[8 * k : 8 * k + 8] for k in range(8)], axis=1)
    top_local = dot(buckets.astype(BF16), m2l_ref[...].reshape(2048, 256)).astype(BF16)
    for c in range(8):
        put_every_eighth(parents_s, c, 4, dot(top_local, l2l_ref[c])[0:4])
    for k in range(8):
        far_z[128 * k : 128 * k + 128, :] = dot(leaf_rows, m2l_ref[k]).astype(BF16)
    parent_local = (par_ref[...] + wide(parents_s[...])).astype(BF16)
    for c in range(8):
        put_every_eighth(leaves_s, c, 32, dot(parent_local, l2l_ref[c]))
    total = partial_ref[...] + dot(far_ref[...], far_z[...])
    local_ref[...] = (total + wide(leaves_s[...])).astype(BF16)

    below = tiles_of(recv_ref[(me + 15) % 16, 16:32, :])
    above = tiles_of(recv_ref[(me + 1) % 16, 16:32, :])
    clear_rows(source_s, 8)
    put_source(source_s, 0, 4, below[0:3])
    put_source(source_s, 4, 4, above[0:3])
    charges = [below[3], above[3]]
    halo = (0, 1, 2, 3, 12, 13, 14, 15)
    near_out_ref[...] = near_ref[...] + near_sum(
        list_ref, lambda t: target_ref[t], side_by_side(source_s), halo, jnp.concatenate(charges, axis=0), total_s
    )


def finish(near_src, targets, near, recv, partial, far, par, top, m2l, l2l):
    return pl.pallas_call(
        finish_kernel,
        out_shape=(jax.ShapeDtypeStruct((256, 256), BF16), jax.ShapeDtypeStruct((8, 128), F32)),
        scratch_shapes=[
            pltpu.VMEM((256, 128), F32),
            pltpu.VMEM((1024, 128), F32),
            pltpu.VMEM((1024, 256), BF16),
            pltpu.VMEM((2, 32, 128), F32),
            pltpu.VMEM((2, 256, 128), F32),
        ],
        compiler_params=pltpu.CompilerParams(vmem_limit_bytes=VMEM_LIMIT),
        cost_estimate=pl.CostEstimate(flops=3_000_000_000, bytes_accessed=3_500_000, transcendentals=1_000_000),
        name="finish",
    )(near_src, targets, near, recv, partial, far, par, top, m2l, l2l)


def shifted(block, axis, distance):
    size = lax.axis_size(axis)
    route = [(i, i + distance) for i in range(size) if 0 <= i + distance < size]
    return lax.ppermute(block, axis, route)


def per_device(
    leaf_moments, leaf_src, leaf_cls, send_rows, send_count, par_src, par_cls, top_src, top_cls,
    points, charges, near_src, m2m_ops, m2l_ops, l2l_ops,
):
    points = points.transpose(1, 0, 2)
    sent, up, down = pack(
        leaf_moments, m2m_ops, send_rows[0].transpose(0, 2, 1), send_count[0], points, charges
    )
    before = shifted(up, "gx", 1)
    after = shifted(down, "gx", -1)
    recv = lax.all_to_all(with_ends(sent, before, after), "gy", 0, 0, tiled=True)
    partial, far, par, top = lists(
        leaf_moments, m2l_ops, before, up, after,
        leaf_src.T, leaf_cls.T, par_src, par_cls, top_src.T, top_cls.T,
    )
    near_own, targets = own_tiles(par, near_src, points, charges)
    return finish(near_src, targets, near_own, recv, partial, far, par, top, m2l_ops, l2l_ops)


def solution(mesh):
    both = P(("gx", "gy"))
    return jax.shard_map(
        per_device,
        mesh=mesh,
        in_specs=(both, both, both, P("gx"), P("gx"), both, both, P("gx"), P("gx"), both, both, both, P(), P(), P()),
        out_specs=(both, both),
        check_vma=False,
    )
```

```python
import jax
import jax.numpy as jnp
from jax import lax
from jax.experimental import pallas as pl
from jax.experimental.pallas import tpu as pltpu
from jax.sharding import PartitionSpec as P

F32 = jnp.float32
BF16 = jnp.bfloat16
I32 = jnp.int32

HALO_T = 4
SOFTENING = 0.05
VMEM_LIMIT = 10 * 1024 * 1024


def iota(shape, dim):
    return lax.broadcasted_iota(I32, shape, dim)


def dot(a, b):
    return jnp.dot(a, b, preferred_element_type=F32)


def dot_nt(a, b):
    return lax.dot_general(a, b, (((1,), (1,)), ((), ())), preferred_element_type=F32)


def dot_tn(a, b):
    return lax.dot_general(a, b, (((0,), (0,)), ((), ())), preferred_element_type=F32)


def pieces(x):
    high = x.astype(BF16).astype(F32)
    rest = x - high
    middle = rest.astype(BF16).astype(F32)
    return high, middle, rest - middle


def wide(value):
    return jnp.concatenate([value[0], value[1]], axis=1)


def every_eighth(ref, first, count):
    return wide([ref[half, pl.ds(first, count, stride=8), :] for half in range(2)])


def put_every_eighth(ref, first, count, value):
    for half in range(2):
        ref[half, pl.ds(first, count, stride=8), :] = value[:, 128 * half : 128 * half + 128]


def fetch(copies):
    for copy in copies:
        copy.start()
    return copies


def tile_rows(parts, first):
    high = jnp.concatenate([part[0][first : first + HALO_T] for part in parts], axis=0)
    rest = jnp.concatenate([part[1][first : first + HALO_T] for part in parts], axis=0)
    return jnp.concatenate([high, rest], axis=1)


def pack_kernel(
    leaf_hbm, m2m_hbm, rows_hbm, count_hbm, points_hbm, charges_hbm, send_ref, up_ref, down_ref, m2m_ref,
    leaf_ref, rows_ref, count_ref, points_ref, charges_ref, leaf_s, sems,
):
    me = lax.axis_index("gy")
    pairs = (
        (leaf_hbm, leaf_ref), (rows_hbm.at[me], rows_ref), (count_hbm, count_ref),
        (points_hbm, points_ref), (charges_hbm, charges_ref), (m2m_hbm, m2m_ref),
    )
    copies = fetch([pltpu.make_async_copy(a, b, sems.at[i]) for i, (a, b) in enumerate(pairs)])
    for copy in copies[:5]:
        copy.wait()
    leaf = leaf_ref[...]
    for half in range(2):
        leaf_s[half] = leaf[:, 128 * half : 128 * half + 128].astype(F32)
    table = rows_ref[...].astype(F32)
    live = iota((8, 16), 0) < count_ref[pl.ds(me, 1), :]
    table = jnp.where(live, table, -1.0).astype(BF16)
    repeat = (iota((128, 16), 0) // 8 == iota((128, 16), 1)).astype(F32).astype(BF16)
    spread = dot_nt(repeat, table)
    column = jnp.sum(
        jnp.where(iota((128, 8), 0) % 8 == iota((128, 8), 1), spread, 0.0), axis=1, keepdims=True
    )
    pick = (iota((128, 256), 1).astype(F32) == column).astype(F32).astype(BF16)
    sent = dot(pick, leaf)
    parts = [pieces(x) for x in (points_ref[0], points_ref[1], points_ref[2], charges_ref[...])]
    first = tile_rows(parts, 0)
    last = tile_rows(parts, 8 - HALO_T)
    for p in range(16):
        tiles = jnp.where(me + 1 == p, last, jnp.where(me - 1 == p, first, 0.0))
        rows = jnp.concatenate([sent[8 * p : 8 * p + 8], jnp.zeros((8, 256), F32), tiles], axis=0)
        send_ref[p] = rows.astype(BF16)
    up_ref[32:48, :] = last.astype(BF16)
    down_ref[32:48, :] = first.astype(BF16)
    copies[5].wait()
    operators = m2m_ref[...].reshape(2048, 256)
    children = jnp.concatenate([every_eighth(leaf_s, c, 32) for c in range(8)], axis=1)
    parents = dot(children.astype(BF16), operators).astype(BF16)
    up_ref[0:32, :] = parents
    down_ref[0:32, :] = parents


def pack(leaf, m2m, rows, count, points, charges):
    return pl.pallas_call(
        pack_kernel,
        out_shape=(
            jax.ShapeDtypeStruct((16, 32, 256), BF16),
            jax.ShapeDtypeStruct((48, 256), BF16),
            jax.ShapeDtypeStruct((48, 256), BF16),
            jax.ShapeDtypeStruct((8, 256, 256), BF16),
        ),
        in_specs=[pl.BlockSpec(memory_space=pltpu.HBM)] * 6,
        scratch_shapes=[
            pltpu.VMEM((256, 256), BF16),
            pltpu.VMEM((8, 16), I32),
            pltpu.VMEM((16, 16), I32),
            pltpu.VMEM((3, 8, 128), F32),
            pltpu.VMEM((8, 128), F32),
            pltpu.VMEM((2, 256, 128), F32),
            pltpu.SemaphoreType.DMA((6,)),
        ],
        compiler_params=pltpu.CompilerParams(vmem_limit_bytes=VMEM_LIMIT),
        cost_estimate=pl.CostEstimate(flops=200_000_000, bytes_accessed=1_500_000, transcendentals=0),
        name="pack",
    )(*[pltpu.with_memory_space_constraint(x, pltpu.HBM) for x in (leaf, m2m, rows, count, points, charges)])


def tops_kernel(up_ref, m2m_ref, top_ref, parents_s):
    parents = up_ref[0:32, :].astype(F32)
    for half in range(2):
        parents_s[half, 0:32, :] = parents[:, 128 * half : 128 * half + 128]
        parents_s[half, 32:64, :] = jnp.zeros((32, 128), F32)
    children = jnp.concatenate([every_eighth(parents_s, c, 8) for c in range(8)], axis=1)
    top_ref[...] = dot(children.astype(BF16), m2m_ref[...].reshape(2048, 256))


def tops(up, m2m):
    return pl.pallas_call(
        tops_kernel,
        out_shape=jax.ShapeDtypeStruct((8, 256), F32),
        scratch_shapes=[pltpu.VMEM((2, 64, 128), F32)],
        compiler_params=pltpu.CompilerParams(vmem_limit_bytes=VMEM_LIMIT),
        cost_estimate=pl.CostEstimate(flops=100_000_000, bytes_accessed=1_100_000, transcendentals=0),
        name="tops",
    )(up, m2m)


def ends_kernel(send_ref, top_ref, before_ref, after_ref, out_ref):
    me = lax.axis_index("gy")
    top = jnp.concatenate([jnp.zeros((8, 256), F32), top_ref[...], jnp.zeros((16, 256), F32)], axis=0).astype(BF16)
    for p in range(16):
        out_ref[p] = send_ref[p] + top

    @pl.when(me == 15)
    def _():
        out_ref[0, 16:32, :] = before_ref[32:48, :]

    @pl.when(me == 0)
    def _():
        out_ref[15, 16:32, :] = after_ref[32:48, :]


def with_ends(send, top, before, after):
    return pl.pallas_call(
        ends_kernel,
        out_shape=jax.ShapeDtypeStruct((16, 32, 256), BF16),
        compiler_params=pltpu.CompilerParams(vmem_limit_bytes=VMEM_LIMIT),
        name="with_ends",
    )(send, top, before, after)


def fields(src_ref, val_ref, lanes, base, rows):
    at = iota((rows, 128), 0)
    even = jnp.zeros((rows, 128), I32)
    odd = jnp.zeros((rows, 128), I32)
    for first, last in ((0, 15), (15, 30), (30, 32)):
        word = jnp.zeros((rows, 128), I32)
        for j in range(first, last):
            hit = at == (src_ref[j : j + 1, lanes] - base)
            word += jnp.where(hit, val_ref[j : j + 1, lanes], 0)
        even += word & 0x0F0F0F0F
        odd += (word >> 4) & 0x0F0F0F0F
    return even, odd


def counts_of(even, odd, k):
    word = odd if k % 2 else even
    return ((word >> (8 * (k // 2))) & 0xFF).astype(F32).astype(BF16)


def field_of(cls):
    return jnp.where(cls >= 0, jnp.left_shift(1, 4 * jnp.maximum(cls, 0)), 0)


def lists_kernel(
    leaf_ref, m2l_ref, before_ref, parents_ref, after_ref, src_hbm, cls_hbm, par_src_hbm, par_cls_hbm, top_src_hbm, top_cls_hbm,
    partial_ref, far_ref, par_ref, top_ref,
    src_t, val_t, low_src, low_val, par_src_ref, par_cls_ref, top_src_ref, top_cls_ref, near_w, far_w, z_ref, small_w, par_z, sems,
):
    me = lax.axis_index("gy")
    device = lax.axis_index("gx") * 16 + me
    pairs = (
        (src_hbm, src_t), (cls_hbm, val_t), (par_src_hbm, par_src_ref), (par_cls_hbm, par_cls_ref),
        (top_src_hbm, top_src_ref), (top_cls_hbm, top_cls_ref),
    )
    copies = fetch([pltpu.make_async_copy(a, b, sems.at[i]) for i, (a, b) in enumerate(pairs)])
    leaf = leaf_ref[...]
    for k in range(8):
        z_ref[256 * k : 256 * k + 256, :] = dot(leaf, m2l_ref[k]).astype(BF16)
    bank = jnp.concatenate([before_ref[0:32, :], parents_ref[0:32, :], after_ref[0:32, :]], axis=0)
    for k in range(8):
        z = dot(bank, m2l_ref[k])
        par_z[128 * k : 128 * k + 128, :] = jnp.concatenate([z, jnp.zeros((32, 256), F32)], axis=0).astype(BF16)
    for copy in copies:
        copy.wait()
    src = src_t[...]
    src_t[...] = jnp.where(src >= 4096, src - (4096 - 256), src - 256 * me)
    val_t[...] = field_of(val_t[...])
    src = par_src_ref[...]
    place = (src // 32 - device + 16) // 16
    src = jnp.where(src >= 0, place * 32 + src % 32, -1)
    none = jnp.full((96, 32), -1, I32)
    src = jnp.concatenate([src, none], axis=0).T
    cls = jnp.concatenate([par_cls_ref[...], none], axis=0).T
    top = top_src_ref[...]
    top = jnp.where(top >= 0, (top // 4) * 8 + top % 4, -1)
    none = jnp.full((32, 32), -1, I32)
    low_src[...] = jnp.concatenate([src[:, 0:32], top, none], axis=1)
    low_val[...] = field_of(jnp.concatenate([cls[:, 0:32], top_cls_ref[...], none], axis=1))

    rows = 64

    def near_block(i, _):
        for half in range(2):
            lanes = slice(128 * half, 128 * half + 128)
            even, odd = fields(src_t, val_t, lanes, i * rows, rows)
            for k in range(8):
                near_w[pl.ds(pl.multiple_of(256 * k + i * rows, rows), rows), lanes] = counts_of(even, odd, k)
        return 0

    def far_block(i, _):
        for half in range(2):
            lanes = slice(128 * half, 128 * half + 128)
            even, odd = fields(src_t, val_t, lanes, 256 + i * rows, rows)
            for k in range(8):
                far_w[pl.ds(pl.multiple_of(128 * k + i * rows, rows), rows), lanes] = counts_of(even, odd, k)
        return 0

    def small_block(i, _):
        even, odd = fields(low_src, low_val, slice(0, 128), i * rows, rows)
        for k in range(8):
            small_w[pl.ds(pl.multiple_of(128 * k + i * rows, rows), rows), :] = counts_of(even, odd, k)
        return 0

    lax.fori_loop(0, 4, near_block, 0)
    lax.fori_loop(0, 2, far_block, 0)
    lax.fori_loop(0, 2, small_block, 0)
    partial_ref[...] = dot_tn(near_w[...], z_ref[...])
    for k in range(8):
        far_ref[:, 128 * k : 128 * k + 128] = far_w[128 * k : 128 * k + 128, :].T
    weights = small_w[...].T
    own = (iota((8, 128), 1) == 32 + 4 * me + iota((8, 128), 0)) & (iota((8, 128), 0) < 4)
    own = dot(own.astype(F32).astype(BF16), weights)
    top_ref[...] = jnp.concatenate([own[:, 128 * k : 128 * k + 128] for k in range(8)], axis=0).astype(BF16)
    par_ref[...] = dot(weights[0:32], par_z[...])


def lists(leaf, m2l, before, parents, after, src, cls, par_src, par_cls, top_src, top_cls):
    vmem = pl.BlockSpec(memory_space=pltpu.VMEM)
    return pl.pallas_call(
        lists_kernel,
        out_shape=(
            jax.ShapeDtypeStruct((256, 256), F32),
            jax.ShapeDtypeStruct((256, 1024), BF16),
            jax.ShapeDtypeStruct((32, 256), F32),
            jax.ShapeDtypeStruct((64, 128), BF16),
        ),
        in_specs=[vmem] * 5 + [pl.BlockSpec(memory_space=pltpu.HBM)] * 6,
        scratch_shapes=[
            pltpu.VMEM((32, 256), I32),
            pltpu.VMEM((32, 256), I32),
            pltpu.VMEM((32, 128), I32),
            pltpu.VMEM((32, 128), I32),
            pltpu.VMEM((32, 32), I32),
            pltpu.VMEM((32, 32), I32),
            pltpu.VMEM((32, 64), I32),
            pltpu.VMEM((32, 64), I32),
            pltpu.VMEM((2048, 256), BF16),
            pltpu.VMEM((1024, 256), BF16),
            pltpu.VMEM((2048, 256), BF16),
            pltpu.VMEM((1024, 128), BF16),
            pltpu.VMEM((1024, 256), BF16),
            pltpu.SemaphoreType.DMA((6,)),
        ],
        compiler_params=pltpu.CompilerParams(vmem_limit_bytes=VMEM_LIMIT),
        cost_estimate=pl.CostEstimate(flops=4_000_000_000, bytes_accessed=2_500_000, transcendentals=0),
        name="lists",
    )(leaf, m2l, before, parents, after, src, cls, par_src, par_cls, top_src, top_cls)


def put_rows(ref, first, count, row, value):
    ref[pl.ds(32 * first + row, count, stride=32), :] = value


def put_source(ref, first, count, xyz):
    split = [pieces(x) for x in xyz]
    for row, kind in enumerate((0, 0, 1, 0, 2, 1)):
        for axis in range(3):
            put_rows(ref, first, count, 3 * row + axis, split[axis][kind])
    norm = xyz[0] * xyz[0] + xyz[1] * xyz[1] + xyz[2] * xyz[2]
    for i, part in enumerate(pieces(norm)):
        put_rows(ref, first, count, 18 + i, jnp.ones((count, 128), F32))
        put_rows(ref, first, count, 21 + i, part)


def put_target(ref, xyz):
    split = [pieces(-2.0 * x) for x in xyz]
    for row, kind in enumerate((0, 1, 0, 2, 0, 1)):
        for axis in range(3):
            put_rows(ref, 0, 8, 3 * row + axis, split[axis][kind])
    norm = xyz[0] * xyz[0] + xyz[1] * xyz[1] + xyz[2] * xyz[2] + SOFTENING * SOFTENING
    for i, part in enumerate(pieces(norm)):
        put_rows(ref, 0, 8, 18 + i, part)
        put_rows(ref, 0, 8, 21 + i, jnp.ones((8, 128), F32))


def clear_rows(ref, tiles):
    for s in range(tiles):
        ref[32 * s + 24 : 32 * s + 32, :] = jnp.zeros((8, 128), F32)


def side_by_side(ref):
    return jnp.concatenate([ref[32 * s : 32 * s + 32, :] for s in range(8)], axis=1).astype(BF16)


def tiles_of(rows):
    rows = rows.astype(F32)
    rows = rows[:, 0:128] + rows[:, 128:256]
    return [rows[4 * i : 4 * i + 4] for i in range(4)]


def near_sum(list_ref, target_of, sources, places, charges, total_s):
    device = lax.axis_index("gx") * 16 + lax.axis_index("gy")
    number = list_ref[...]
    place = jnp.where(number >= 0, number - (device * 8 - HALO_T), -1)
    weights = []
    for i, s in enumerate(places):
        times = jnp.sum((place == s).astype(F32), axis=1, keepdims=True)
        weights.append(times * charges[i : i + 1, :])
    for t in range(8):
        square = dot_tn(target_of(t), sources)
        total = weights[0][t : t + 1, :] * lax.rsqrt(square[:, 0:128])
        for i in range(1, 8):
            total += weights[i][t : t + 1, :] * lax.rsqrt(square[:, 128 * i : 128 * i + 128])
        total_s[128 * t : 128 * t + 128, :] = total
    ones = jnp.ones((8, 128), BF16)
    row = 0.0
    for part in pieces(total_s[...]):
        row += dot_nt(ones, part.astype(BF16))[0:1, :]
    return jnp.concatenate([row[:, 128 * t : 128 * t + 128] for t in range(8)], axis=0)


def own_kernel(
    after_ref, list_ref, points_ref, charges_ref, out_ref, target_ref, source_s, target_s, total_s
):
    xyz = [points_ref[axis] for axis in range(3)]
    clear_rows(source_s, 8)
    clear_rows(target_s, 8)
    put_source(source_s, 0, 8, xyz)
    put_target(target_s, xyz)
    for t in range(8):
        target_ref[t] = target_s[32 * t : 32 * t + 32, :].astype(BF16)
    own = range(HALO_T, HALO_T + 8)
    out_ref[...] = near_sum(
        list_ref, lambda t: target_ref[t], side_by_side(source_s), own, charges_ref[...], total_s
    )


def own_tiles(after, near_src, points, charges):
    return pl.pallas_call(
        own_kernel,
        out_shape=(
            jax.ShapeDtypeStruct((8, 128), F32),
            jax.ShapeDtypeStruct((8, 32, 128), BF16),
        ),
        scratch_shapes=[
            pltpu.VMEM((256, 128), F32),
            pltpu.VMEM((256, 128), F32),
            pltpu.VMEM((1024, 128), F32),
        ],
        compiler_params=pltpu.CompilerParams(vmem_limit_bytes=VMEM_LIMIT),
        cost_estimate=pl.CostEstimate(flops=2_000_000_000, bytes_accessed=100_000, transcendentals=1_000_000),
        name="own_tiles",
    )(after, near_src, points, charges)


def finish_kernel(
    list_ref, target_ref, near_ref, recv_ref, partial_ref, far_ref, par_ref, top_ref, m2l_ref, l2l_ref,
    local_ref, near_out_ref, source_s, total_s, far_z, parents_s, leaves_s,
):
    me = lax.axis_index("gy")
    rows = recv_ref[:, 0:16, :].astype(F32)
    leaf_rows = rows[:, 0:8].reshape(128, 256).astype(BF16)
    top_rows = rows[:, 8:16].reshape(128, 256).astype(BF16)
    buckets = dot(top_ref[...], top_rows).astype(BF16).astype(F32)
    buckets = jnp.concatenate([buckets[8 * k : 8 * k + 8] for k in range(8)], axis=1)
    top_local = dot(buckets.astype(BF16), m2l_ref[...].reshape(2048, 256)).astype(BF16)
    for c in range(8):
        put_every_eighth(parents_s, c, 4, dot(top_local, l2l_ref[c])[0:4])
    for k in range(8):
        far_z[128 * k : 128 * k + 128, :] = dot(leaf_rows, m2l_ref[k]).astype(BF16)
    parent_local = (par_ref[...] + wide(parents_s[...])).astype(BF16)
    for c in range(8):
        put_every_eighth(leaves_s, c, 32, dot(parent_local, l2l_ref[c]))
    total = partial_ref[...] + dot(far_ref[...], far_z[...])
    local_ref[...] = (total + wide(leaves_s[...])).astype(BF16)

    below = tiles_of(recv_ref[(me + 15) % 16, 16:32, :])
    above = tiles_of(recv_ref[(me + 1) % 16, 16:32, :])
    clear_rows(source_s, 8)
    put_source(source_s, 0, 4, below[0:3])
    put_source(source_s, 4, 4, above[0:3])
    charges = [below[3], above[3]]
    halo = (0, 1, 2, 3, 12, 13, 14, 15)
    near_out_ref[...] = near_ref[...] + near_sum(
        list_ref, lambda t: target_ref[t], side_by_side(source_s), halo, jnp.concatenate(charges, axis=0), total_s
    )


def finish(near_src, targets, near, recv, partial, far, par, top, m2l, l2l):
    return pl.pallas_call(
        finish_kernel,
        out_shape=(jax.ShapeDtypeStruct((256, 256), BF16), jax.ShapeDtypeStruct((8, 128), F32)),
        scratch_shapes=[
            pltpu.VMEM((256, 128), F32),
            pltpu.VMEM((1024, 128), F32),
            pltpu.VMEM((1024, 256), BF16),
            pltpu.VMEM((2, 32, 128), F32),
            pltpu.VMEM((2, 256, 128), F32),
        ],
        compiler_params=pltpu.CompilerParams(vmem_limit_bytes=VMEM_LIMIT),
        cost_estimate=pl.CostEstimate(flops=3_000_000_000, bytes_accessed=3_500_000, transcendentals=1_000_000),
        name="finish",
    )(near_src, targets, near, recv, partial, far, par, top, m2l, l2l)


def shifted(block, axis, distance):
    size = lax.axis_size(axis)
    route = [(i, i + distance) for i in range(size) if 0 <= i + distance < size]
    return lax.ppermute(block, axis, route)


def per_device(
    leaf_moments, leaf_src, leaf_cls, send_rows, send_count, par_src, par_cls, top_src, top_cls,
    points, charges, near_src, m2m_ops, m2l_ops, l2l_ops,
):
    points = points.transpose(1, 0, 2)
    sent, up, down, m2m = pack(
        leaf_moments, m2m_ops, send_rows[0].transpose(0, 2, 1), send_count[0], points, charges
    )
    before = shifted(up, "gx", 1)
    after = shifted(down, "gx", -1)
    recv = lax.all_to_all(with_ends(sent, tops(up, m2m), before, after), "gy", 0, 0, tiled=True)
    partial, far, par, top = lists(
        leaf_moments, m2l_ops, before, up, after,
        leaf_src.T, leaf_cls.T, par_src, par_cls, top_src.T, top_cls.T,
    )
    near_own, targets = own_tiles(par, near_src, points, charges)
    return finish(near_src, targets, near_own, recv, partial, far, par, top, m2l_ops, l2l_ops)


def solution(mesh):
    both = P(("gx", "gy"))
    return jax.shard_map(
        per_device,
        mesh=mesh,
        in_specs=(both, both, both, P("gx"), P("gx"), both, both, P("gx"), P("gx"), both, both, both, P(), P(), P()),
        out_specs=(both, both),
        check_vma=False,
    )
```

```python
import jax
import jax.numpy as jnp
from jax import lax
from jax.experimental import pallas as pl
from jax.experimental.pallas import tpu as pltpu
from jax.sharding import PartitionSpec as P

F32 = jnp.float32
BF16 = jnp.bfloat16
I32 = jnp.int32

HALO_T = 4
SOFTENING = 0.05
VMEM_LIMIT = 10 * 1024 * 1024


def iota(shape, dim):
    return lax.broadcasted_iota(I32, shape, dim)


def dot(a, b):
    return jnp.dot(a, b, preferred_element_type=F32)


def dot_nt(a, b):
    return lax.dot_general(a, b, (((1,), (1,)), ((), ())), preferred_element_type=F32)


def dot_tn(a, b):
    return lax.dot_general(a, b, (((0,), (0,)), ((), ())), preferred_element_type=F32)


def pieces(x):
    high = x.astype(BF16).astype(F32)
    rest = x - high
    middle = rest.astype(BF16).astype(F32)
    return high, middle, rest - middle


def wide(value):
    return jnp.concatenate([value[0], value[1]], axis=1)


def every_eighth(ref, first, count):
    return wide([ref[half, pl.ds(first, count, stride=8), :] for half in range(2)])


def put_every_eighth(ref, first, count, value):
    for half in range(2):
        ref[half, pl.ds(first, count, stride=8), :] = value[:, 128 * half : 128 * half + 128]


def fetch(copies):
    for copy in copies:
        copy.start()
    return copies


def tile_rows(parts, first):
    high = jnp.concatenate([part[0][first : first + HALO_T] for part in parts], axis=0)
    rest = jnp.concatenate([part[1][first : first + HALO_T] for part in parts], axis=0)
    return jnp.concatenate([high, rest], axis=1)


def pack_kernel(
    leaf_hbm, m2m_hbm, rows_hbm, count_hbm, points_hbm, charges_hbm, send_ref, up_ref, down_ref, m2m_ref,
    leaf_ref, rows_ref, count_ref, points_ref, charges_ref, leaf_s, sems,
):
    me = lax.axis_index("gy")
    pairs = (
        (leaf_hbm, leaf_ref), (rows_hbm.at[me], rows_ref), (count_hbm, count_ref),
        (points_hbm, points_ref), (charges_hbm, charges_ref), (m2m_hbm, m2m_ref),
    )
    copies = fetch([pltpu.make_async_copy(a, b, sems.at[i]) for i, (a, b) in enumerate(pairs)])
    for copy in copies[:5]:
        copy.wait()
    leaf = leaf_ref[...]
    for half in range(2):
        leaf_s[half] = leaf[:, 128 * half : 128 * half + 128].astype(F32)
    table = rows_ref[...].astype(F32)
    live = iota((8, 16), 0) < count_ref[pl.ds(me, 1), :]
    table = jnp.where(live, table, -1.0).astype(BF16)
    repeat = (iota((128, 16), 0) // 8 == iota((128, 16), 1)).astype(F32).astype(BF16)
    spread = dot_nt(repeat, table)
    column = jnp.sum(
        jnp.where(iota((128, 8), 0) % 8 == iota((128, 8), 1), spread, 0.0), axis=1, keepdims=True
    )
    pick = (iota((128, 256), 1).astype(F32) == column).astype(F32).astype(BF16)
    sent = dot(pick, leaf)
    parts = [pieces(x) for x in (points_ref[0], points_ref[1], points_ref[2], charges_ref[...])]
    first = tile_rows(parts, 0)
    last = tile_rows(parts, 8 - HALO_T)
    for p in range(16):
        tiles = jnp.where(me + 1 == p, last, jnp.where(me - 1 == p, first, 0.0))
        rows = jnp.concatenate([sent[8 * p : 8 * p + 8], jnp.zeros((8, 256), F32), tiles], axis=0)
        send_ref[p] = rows.astype(BF16)
    up_ref[32:48, :] = last.astype(BF16)
    down_ref[32:48, :] = first.astype(BF16)
    copies[5].wait()
    operators = m2m_ref[...].reshape(2048, 256)
    children = jnp.concatenate([every_eighth(leaf_s, c, 32) for c in range(8)], axis=1)
    parents = dot(children.astype(BF16), operators).astype(BF16)
    up_ref[0:32, :] = parents
    down_ref[0:32, :] = parents


def pack(leaf, m2m, rows, count, points, charges):
    return pl.pallas_call(
        pack_kernel,
        out_shape=(
            jax.ShapeDtypeStruct((16, 32, 256), BF16),
            jax.ShapeDtypeStruct((48, 256), BF16),
            jax.ShapeDtypeStruct((48, 256), BF16),
            jax.ShapeDtypeStruct((8, 256, 256), BF16),
        ),
        in_specs=[pl.BlockSpec(memory_space=pltpu.HBM)] * 6,
        scratch_shapes=[
            pltpu.VMEM((256, 256), BF16),
            pltpu.VMEM((8, 16), I32),
            pltpu.VMEM((16, 16), I32),
            pltpu.VMEM((3, 8, 128), F32),
            pltpu.VMEM((8, 128), F32),
            pltpu.VMEM((2, 256, 128), F32),
            pltpu.SemaphoreType.DMA((6,)),
        ],
        compiler_params=pltpu.CompilerParams(vmem_limit_bytes=VMEM_LIMIT),
        cost_estimate=pl.CostEstimate(flops=200_000_000, bytes_accessed=1_500_000, transcendentals=0),
        name="pack",
    )(*[pltpu.with_memory_space_constraint(x, pltpu.HBM) for x in (leaf, m2m, rows, count, points, charges)])


def tops_kernel(up_ref, m2m_ref, top_ref, parents_s):
    parents = up_ref[0:32, :].astype(F32)
    for half in range(2):
        parents_s[half, 0:32, :] = parents[:, 128 * half : 128 * half + 128]
        parents_s[half, 32:64, :] = jnp.zeros((32, 128), F32)
    children = jnp.concatenate([every_eighth(parents_s, c, 8) for c in range(8)], axis=1)
    top_ref[...] = dot(children.astype(BF16), m2m_ref[...].reshape(2048, 256))


def tops(up, m2m):
    return pl.pallas_call(
        tops_kernel,
        out_shape=jax.ShapeDtypeStruct((8, 256), F32),
        scratch_shapes=[pltpu.VMEM((2, 64, 128), F32)],
        compiler_params=pltpu.CompilerParams(vmem_limit_bytes=VMEM_LIMIT),
        cost_estimate=pl.CostEstimate(flops=100_000_000, bytes_accessed=1_100_000, transcendentals=0),
        name="tops",
    )(up, m2m)


def ends_kernel(send_ref, top_ref, before_ref, after_ref, out_ref):
    me = lax.axis_index("gy")
    top = jnp.concatenate([jnp.zeros((8, 256), F32), top_ref[...], jnp.zeros((16, 256), F32)], axis=0).astype(BF16)
    for p in range(16):
        out_ref[p] = send_ref[p] + top

    @pl.when(me == 15)
    def _():
        out_ref[0, 16:32, :] = before_ref[32:48, :]

    @pl.when(me == 0)
    def _():
        out_ref[15, 16:32, :] = after_ref[32:48, :]


def with_ends(send, top, before, after):
    return pl.pallas_call(
        ends_kernel,
        out_shape=jax.ShapeDtypeStruct((16, 32, 256), BF16),
        compiler_params=pltpu.CompilerParams(vmem_limit_bytes=VMEM_LIMIT),
        name="with_ends",
    )(send, top, before, after)


def fields(src_ref, val_ref, lanes, base, rows):
    at = iota((rows, 128), 0)
    even = jnp.zeros((rows, 128), I32)
    odd = jnp.zeros((rows, 128), I32)
    for first, last in ((0, 15), (15, 30), (30, 32)):
        word = jnp.zeros((rows, 128), I32)
        for j in range(first, last):
            hit = at == (src_ref[j : j + 1, lanes] - base)
            word += jnp.where(hit, val_ref[j : j + 1, lanes], 0)
        even += word & 0x0F0F0F0F
        odd += (word >> 4) & 0x0F0F0F0F
    return even, odd


def counts_of(even, odd, k):
    word = odd if k % 2 else even
    return ((word >> (8 * (k // 2))) & 0xFF).astype(F32).astype(BF16)


def field_of(cls):
    return jnp.where(cls >= 0, jnp.left_shift(1, 4 * jnp.maximum(cls, 0)), 0)


def lists_kernel(
    leaf_ref, m2l_ref, before_ref, parents_ref, after_ref, src_hbm, cls_hbm, par_src_hbm, par_cls_hbm, top_src_hbm, top_cls_hbm,
    partial_ref, far_ref, par_ref, top_ref,
    src_t, val_t, low_src, low_val, par_src_ref, par_cls_ref, top_src_ref, top_cls_ref, near_w, far_w, z_ref, small_w, par_z, sems,
):
    me = lax.axis_index("gy")
    device = lax.axis_index("gx") * 16 + me
    pairs = (
        (src_hbm, src_t), (cls_hbm, val_t), (par_src_hbm, par_src_ref), (par_cls_hbm, par_cls_ref),
        (top_src_hbm, top_src_ref), (top_cls_hbm, top_cls_ref),
    )
    copies = fetch([pltpu.make_async_copy(a, b, sems.at[i]) for i, (a, b) in enumerate(pairs)])
    leaf = leaf_ref[...]
    for k in range(8):
        z_ref[256 * k : 256 * k + 256, :] = dot(leaf, m2l_ref[k]).astype(BF16)
    bank = jnp.concatenate([before_ref[0:32, :], parents_ref[0:32, :], after_ref[0:32, :]], axis=0)
    for k in range(8):
        z = dot(bank, m2l_ref[k])
        par_z[128 * k : 128 * k + 128, :] = jnp.concatenate([z, jnp.zeros((32, 256), F32)], axis=0).astype(BF16)
    for copy in copies:
        copy.wait()
    src = src_t[...]
    src_t[...] = jnp.where(src >= 4096, src - (4096 - 256), src - 256 * me)
    val_t[...] = field_of(val_t[...])
    src = par_src_ref[...]
    place = (src // 32 - device + 16) // 16
    src = jnp.where(src >= 0, place * 32 + src % 32, -1)
    none = jnp.full((96, 32), -1, I32)
    src = jnp.concatenate([src, none], axis=0).T
    cls = jnp.concatenate([par_cls_ref[...], none], axis=0).T
    top = top_src_ref[...]
    top = jnp.where(top >= 0, (top // 4) * 8 + top % 4, -1)
    none = jnp.full((32, 32), -1, I32)
    low_src[...] = jnp.concatenate([src[:, 0:32], top, none], axis=1)
    low_val[...] = field_of(jnp.concatenate([cls[:, 0:32], top_cls_ref[...], none], axis=1))

    rows = 64

    def near_block(i, _):
        for half in range(2):
            lanes = slice(128 * half, 128 * half + 128)
            even, odd = fields(src_t, val_t, lanes, i * rows, rows)
            for k in range(8):
                near_w[pl.ds(pl.multiple_of(256 * k + i * rows, rows), rows), lanes] = counts_of(even, odd, k)
        return 0

    def far_block(i, _):
        for half in range(2):
            lanes = slice(128 * half, 128 * half + 128)
            even, odd = fields(src_t, val_t, lanes, 256 + i * rows, rows)
            for k in range(8):
                far_w[pl.ds(pl.multiple_of(128 * k + i * rows, rows), rows), lanes] = counts_of(even, odd, k)
        return 0

    def small_block(i, _):
        even, odd = fields(low_src, low_val, slice(0, 128), i * rows, rows)
        for k in range(8):
            small_w[pl.ds(pl.multiple_of(128 * k + i * rows, rows), rows), :] = counts_of(even, odd, k)
        return 0

    lax.fori_loop(0, 4, near_block, 0)
    lax.fori_loop(0, 2, far_block, 0)
    lax.fori_loop(0, 2, small_block, 0)
    partial_ref[...] = dot_tn(near_w[...], z_ref[...])
    for k in range(8):
        far_ref[:, 128 * k : 128 * k + 128] = far_w[128 * k : 128 * k + 128, :].T
    weights = small_w[...].T
    own = (iota((8, 128), 1) == 32 + 4 * me + iota((8, 128), 0)) & (iota((8, 128), 0) < 4)
    own = dot(own.astype(F32).astype(BF16), weights)
    top_ref[...] = jnp.concatenate([own[:, 128 * k : 128 * k + 128] for k in range(8)], axis=0).astype(BF16)
    par_ref[...] = dot(weights[0:32], par_z[...])


def lists(leaf, m2l, before, parents, after, src, cls, par_src, par_cls, top_src, top_cls):
    vmem = pl.BlockSpec(memory_space=pltpu.VMEM)
    return pl.pallas_call(
        lists_kernel,
        out_shape=(
            jax.ShapeDtypeStruct((256, 256), F32),
            jax.ShapeDtypeStruct((256, 1024), BF16),
            jax.ShapeDtypeStruct((32, 256), F32),
            jax.ShapeDtypeStruct((64, 128), BF16),
        ),
        in_specs=[vmem] * 5 + [pl.BlockSpec(memory_space=pltpu.HBM)] * 6,
        scratch_shapes=[
            pltpu.VMEM((32, 256), I32),
            pltpu.VMEM((32, 256), I32),
            pltpu.VMEM((32, 128), I32),
            pltpu.VMEM((32, 128), I32),
            pltpu.VMEM((32, 32), I32),
            pltpu.VMEM((32, 32), I32),
            pltpu.VMEM((32, 64), I32),
            pltpu.VMEM((32, 64), I32),
            pltpu.VMEM((2048, 256), BF16),
            pltpu.VMEM((1024, 256), BF16),
            pltpu.VMEM((2048, 256), BF16),
            pltpu.VMEM((1024, 128), BF16),
            pltpu.VMEM((1024, 256), BF16),
            pltpu.SemaphoreType.DMA((6,)),
        ],
        compiler_params=pltpu.CompilerParams(vmem_limit_bytes=VMEM_LIMIT),
        cost_estimate=pl.CostEstimate(flops=4_000_000_000, bytes_accessed=2_500_000, transcendentals=0),
        name="lists",
    )(leaf, m2l, before, parents, after, src, cls, par_src, par_cls, top_src, top_cls)


def put_rows(ref, first, count, row, value):
    ref[pl.ds(32 * first + row, count, stride=32), :] = value


def put_source(ref, first, count, xyz):
    split = [pieces(x) for x in xyz]
    for row, kind in enumerate((0, 0, 1, 0, 2, 1)):
        for axis in range(3):
            put_rows(ref, first, count, 3 * row + axis, split[axis][kind])
    norm = xyz[0] * xyz[0] + xyz[1] * xyz[1] + xyz[2] * xyz[2]
    for i, part in enumerate(pieces(norm)):
        put_rows(ref, first, count, 18 + i, jnp.ones((count, 128), F32))
        put_rows(ref, first, count, 21 + i, part)


def put_target(ref, xyz):
    split = [pieces(-2.0 * x) for x in xyz]
    for row, kind in enumerate((0, 1, 0, 2, 0, 1)):
        for axis in range(3):
            put_rows(ref, 0, 8, 3 * row + axis, split[axis][kind])
    norm = xyz[0] * xyz[0] + xyz[1] * xyz[1] + xyz[2] * xyz[2] + SOFTENING * SOFTENING
    for i, part in enumerate(pieces(norm)):
        put_rows(ref, 0, 8, 18 + i, part)
        put_rows(ref, 0, 8, 21 + i, jnp.ones((8, 128), F32))


def clear_rows(ref, tiles):
    for s in range(tiles):
        ref[32 * s + 24 : 32 * s + 32, :] = jnp.zeros((8, 128), F32)


def side_by_side(ref):
    return jnp.concatenate([ref[32 * s : 32 * s + 32, :] for s in range(8)], axis=1).astype(BF16)


def tiles_of(rows):
    rows = rows.astype(F32)
    rows = rows[:, 0:128] + rows[:, 128:256]
    return [rows[4 * i : 4 * i + 4] for i in range(4)]


def near_sum(list_ref, target_of, sources, places, charges, total_s):
    device = lax.axis_index("gx") * 16 + lax.axis_index("gy")
    number = list_ref[...]
    place = jnp.where(number >= 0, number - (device * 8 - HALO_T), -1)
    weights = []
    for i, s in enumerate(places):
        times = jnp.sum((place == s).astype(F32), axis=1, keepdims=True)
        weights.append(times * charges[i : i + 1, :])
    for t in range(8):
        square = dot_tn(target_of(t), sources)
        total = weights[0][t : t + 1, :] * lax.rsqrt(square[:, 0:128])
        for i in range(1, 8):
            total += weights[i][t : t + 1, :] * lax.rsqrt(square[:, 128 * i : 128 * i + 128])
        total_s[128 * t : 128 * t + 128, :] = total
    ones = jnp.ones((8, 128), BF16)
    row = 0.0
    for part in pieces(total_s[...]):
        row += dot_nt(ones, part.astype(BF16))[0:1, :]
    return jnp.concatenate([row[:, 128 * t : 128 * t + 128] for t in range(8)], axis=0)


def own_kernel(
    after_ref, list_ref, points_ref, charges_ref, out_ref, target_ref, source_s, target_s, total_s
):
    xyz = [points_ref[axis] for axis in range(3)]
    clear_rows(source_s, 8)
    clear_rows(target_s, 8)
    put_source(source_s, 0, 8, xyz)
    put_target(target_s, xyz)
    for t in range(8):
        target_ref[t] = target_s[32 * t : 32 * t + 32, :].astype(BF16)
    own = range(HALO_T, HALO_T + 8)
    out_ref[...] = near_sum(
        list_ref, lambda t: target_ref[t], side_by_side(source_s), own, charges_ref[...], total_s
    )


def own_tiles(after, near_src, points, charges):
    return pl.pallas_call(
        own_kernel,
        out_shape=(
            jax.ShapeDtypeStruct((8, 128), F32),
            jax.ShapeDtypeStruct((8, 32, 128), BF16),
        ),
        scratch_shapes=[
            pltpu.VMEM((256, 128), F32),
            pltpu.VMEM((256, 128), F32),
            pltpu.VMEM((1024, 128), F32),
        ],
        compiler_params=pltpu.CompilerParams(vmem_limit_bytes=VMEM_LIMIT),
        cost_estimate=pl.CostEstimate(flops=2_000_000_000, bytes_accessed=100_000, transcendentals=1_000_000),
        name="own_tiles",
    )(after, near_src, points, charges)


def finish_kernel(
    list_ref, target_ref, near_ref, recv_ref, partial_ref, far_ref, par_ref, top_ref, m2l_ref, l2l_ref,
    local_ref, near_out_ref, source_s, total_s, far_z, parents_s, leaves_s,
):
    me = lax.axis_index("gy")
    rows = recv_ref[:, 0:16, :].astype(F32)
    leaf_rows = rows[:, 0:8].reshape(128, 256).astype(BF16)
    top_rows = rows[:, 8:16].reshape(128, 256).astype(BF16)
    buckets = dot(top_ref[...], top_rows).astype(BF16).astype(F32)
    buckets = jnp.concatenate([buckets[8 * k : 8 * k + 8] for k in range(8)], axis=1)
    top_local = dot(buckets.astype(BF16), m2l_ref[...].reshape(2048, 256)).astype(BF16)
    for c in range(8):
        put_every_eighth(parents_s, c, 4, dot(top_local, l2l_ref[c])[0:4])
    for k in range(8):
        far_z[128 * k : 128 * k + 128, :] = dot(leaf_rows, m2l_ref[k]).astype(BF16)
    parent_local = (par_ref[...] + wide(parents_s[:, 0:32, :])).astype(BF16)
    for c in range(8):
        put_every_eighth(leaves_s, c, 32, dot(parent_local, l2l_ref[c]))
    total = partial_ref[...] + dot(far_ref[...], far_z[...])
    local_ref[...] = (total + wide(leaves_s[...])).astype(BF16)

    below = tiles_of(recv_ref[(me + 15) % 16, 16:32, :])
    above = tiles_of(recv_ref[(me + 1) % 16, 16:32, :])
    clear_rows(source_s, 8)
    put_source(source_s, 0, 4, below[0:3])
    put_source(source_s, 4, 4, above[0:3])
    charges = [below[3], above[3]]
    halo = (0, 1, 2, 3, 12, 13, 14, 15)
    near_out_ref[...] = near_ref[...] + near_sum(
        list_ref, lambda t: target_ref[t], side_by_side(source_s), halo, jnp.concatenate(charges, axis=0), total_s
    )


def finish(near_src, targets, near, recv, partial, far, par, top, m2l, l2l):
    return pl.pallas_call(
        finish_kernel,
        out_shape=(jax.ShapeDtypeStruct((256, 256), BF16), jax.ShapeDtypeStruct((8, 128), F32)),
        scratch_shapes=[
            pltpu.VMEM((384, 128), F32),
            pltpu.VMEM((1024, 128), F32),
            pltpu.VMEM((1024, 256), BF16),
            pltpu.VMEM((2, 64, 128), F32),
            pltpu.VMEM((2, 256, 128), F32),
        ],
        compiler_params=pltpu.CompilerParams(vmem_limit_bytes=VMEM_LIMIT),
        cost_estimate=pl.CostEstimate(flops=3_000_000_000, bytes_accessed=3_500_000, transcendentals=1_000_000),
        name="finish",
    )(near_src, targets, near, recv, partial, far, par, top, m2l, l2l)


def shifted(block, axis, distance):
    size = lax.axis_size(axis)
    route = [(i, i + distance) for i in range(size) if 0 <= i + distance < size]
    return lax.ppermute(block, axis, route)


def per_device(
    leaf_moments, leaf_src, leaf_cls, send_rows, send_count, par_src, par_cls, top_src, top_cls,
    points, charges, near_src, m2m_ops, m2l_ops, l2l_ops,
):
    points = points.transpose(1, 0, 2)
    sent, up, down, m2m = pack(
        leaf_moments, m2m_ops, send_rows[0].transpose(0, 2, 1), send_count[0], points, charges
    )
    before = shifted(up, "gx", 1)
    after = shifted(down, "gx", -1)
    recv = lax.all_to_all(with_ends(sent, tops(up, m2m), before, after), "gy", 0, 0, tiled=True)
    partial, far, par, top = lists(
        leaf_moments, m2l_ops, before, up, after,
        leaf_src.T, leaf_cls.T, par_src, par_cls, top_src.T, top_cls.T,
    )
    near_own, targets = own_tiles(par, near_src, points, charges)
    return finish(near_src, targets, near_own, recv, partial, far, par, top, m2l_ops, l2l_ops)


def solution(mesh):
    both = P(("gx", "gy"))
    return jax.shard_map(
        per_device,
        mesh=mesh,
        in_specs=(both, both, both, P("gx"), P("gx"), both, both, P("gx"), P("gx"), both, both, both, P(), P(), P()),
        out_specs=(both, both),
        check_vma=False,
    )
```
